32 devices in a mesh: gx: 2 (over x), gy: 4 (over y, core), mode: 4 (over z).
Axes of the slice: x: 2, y: 2, z: 4, core: 2. Of those that a mesh axis runs over, the one named last changes fastest.
Arguments:
- e_init: float32 [3, 24, 32, 128], P(None, 'gx', 'gy'), may hold values from -6 to 6
- h_init: float32 [3, 24, 32, 128], P(None, 'gx', 'gy'), may hold values from -6 to 6
- eps_levels: float32 [3], replicated, may hold values from 1 to 4
- region_gain: float32 [3], replicated, may hold values from 0.5 to 2
- region_labels: int32 [24, 32, 128], P('gx', 'gy'), may hold values from 0 to 2
- kl_blocks: bfloat16 [16, 24, 32, 128], P('mode', 'gx', 'gy'), may hold values from -1.5 to 1.5
- kl_modes: int32 [16], replicated, may hold values from 0 to 3, as said below
- source_z: int32 [24, 32], P('gx', 'gy'), may hold values from 0 to 127
- source_amp: float32 [24, 32], P('gx', 'gy'), may hold values from -6 to 6
Outputs:
- tangent_e: float32 [4, 3, 24, 32, 128], P('mode', None, 'gx', 'gy')
- tangent_h: float32 [4, 3, 24, 32, 128], P('mode', None, 'gx', 'gy')
The draws below stay inside these ranges and needn't reach their ends.
Inputs may be any that keep to these rules, and one draw needn't show every extreme that they name: `kl_modes`: each of the 4 modes is named by exactly 4 blocks.
All inputs are finite; a program needn't handle non-finite values.
Results may differ from the reference program's by a relative error of at most 0.00065.
Values may be sent and summed in bfloat16 or wider, within the bound.
No kernel may reach another device: no remote copies, remote signals or barrier semaphores. Data moves between devices by JAX's collectives and lax.ppermute only.
A program may use at most 64 MiB of HBM per device.

```python
import math
import jax
import jax.numpy as jnp

NZ = 128
STEPS = 10
MODES = 4
NKL = 16
NX = 24
NY = 32


def draw_kl_modes(key, part):
    order = jax.random.permutation(key, jnp.arange(NKL, dtype=jnp.int32))
    return (order % MODES).astype(jnp.int32)


def with_ends(drawn, key, least, largest):
    index_at = [jax.random.randint(jax.random.fold_in(key, axis), (), 0, length) for axis, length in enumerate(drawn.shape)]
    longest = drawn.shape.index(max(drawn.shape))
    neighbour = index_at[:longest] + [(index_at[longest] + 1) % drawn.shape[longest]] + index_at[longest + 1:]
    return drawn.at[tuple(index_at)].set(least).at[tuple(neighbour)].set(largest)


def steps_of(stream_key, dims, cuts, low, largest):
    loudness, own = 1.0, jax.random.fold_in(stream_key, 6)
    for axis_at, blocks in cuts:
        steps = jnp.exp(jax.random.uniform(jax.random.fold_in(own, axis_at), (blocks,), jnp.float32, low / len(cuts), largest / len(cuts)))
        loudness = loudness * jnp.repeat(steps, dims[axis_at] // blocks).reshape([-1 if axis == axis_at else 1 for axis in range(len(dims))])
    return loudness


def centred(own_key, dims, scale, most, cuts=(), kind=jnp.bfloat16):
    entries = scale * jax.random.normal(own_key, dims, jnp.float32)
    if cuts:
        entries = entries * steps_of(own_key, dims, cuts, -0.22, 0.18)
    return jnp.clip(entries, -most, most).astype(kind)


def setup_inputs(seed: int = 0) -> dict:
    keys = jax.random.split(jax.random.key(seed), 10)
    return {
        "e_init": centred(keys[0], (3, NX, NY, NZ), 1.0, 6.0, ((1, 2), (2, 4)), jnp.float32),
        "h_init": centred(keys[1], (3, NX, NY, NZ), 1.0, 6.0, ((1, 2), (2, 4)), jnp.float32),
        "eps_levels": jnp.clip(jax.random.uniform(keys[2], (3,), jnp.float32, 1.0, 4.0), 1.0, 4.0),
        "region_gain": jnp.clip(jax.random.uniform(keys[3], (3,), jnp.float32, 0.5, 2.0), 0.5, 2.0),
        "region_labels": with_ends(jax.random.randint(keys[4], (NX, NY, NZ), 0, 3), jax.random.fold_in(keys[4], 1), 0, 2).astype(jnp.int32),
        "kl_blocks": centred(keys[5], (NKL, NX, NY, NZ), 0.25, 1.5, ((0, 4), (1, 2), (2, 4))),
        "kl_modes": draw_kl_modes(jax.random.fold_in(keys[9], 71), 0),
        "source_z": with_ends(jax.random.randint(keys[7], (NX, NY), 0, NZ), jax.random.fold_in(keys[7], 1), 0, NZ - 1).astype(jnp.int32),
        "source_amp": centred(keys[8], (NX, NY), 1.0, 6.0, ((0, 2), (1, 4)), jnp.float32),
    }


DT_STEP = 0.99 / math.sqrt(3.0)
OMEGA_FREQ = 0.7

def pad_wrap(field):
    widths = [(0, 0)] * (field.ndim - 3) + [(1, 1), (1, 1), (0, 0)]
    return jnp.pad(field, widths, mode='wrap')

def curl_forward(padded):
    center = padded[..., 1:-1, 1:-1, :]

    def along_x(component):
        return padded[..., component, 2:, 1:-1, :] - center[..., component, :, :, :]

    def along_y(component):
        return padded[..., component, 1:-1, 2:, :] - center[..., component, :, :, :]

    def along_z(component):
        values = center[..., component, :, :, :]
        return jnp.concatenate([values[..., 1:], jnp.zeros_like(values[..., :1])], -1) - values
    return jnp.stack([along_y(2) - along_z(1), along_z(0) - along_x(2), along_x(1) - along_y(0)], -4)

def curl_backward(padded):
    center = padded[..., 1:-1, 1:-1, :]

    def along_x(component):
        return center[..., component, :, :, :] - padded[..., component, :-2, 1:-1, :]

    def along_y(component):
        return center[..., component, :, :, :] - padded[..., component, 1:-1, :-2, :]

    def along_z(component):
        values = center[..., component, :, :, :]
        return values - jnp.concatenate([jnp.zeros_like(values[..., :1]), values[..., :-1]], -1)
    return jnp.stack([along_y(2) - along_z(1), along_z(0) - along_x(2), along_x(1) - along_y(0)], -4)

def reference(e_init, h_init, eps_levels, region_gain, region_labels, kl_blocks, kl_modes, source_z, source_amp):
    inv_eps = 1.0 / eps_levels[region_labels]
    select = (kl_modes[None, :] == jnp.arange(MODES, dtype=jnp.int32)[:, None]).astype(jnp.float32)
    summed = jnp.einsum('mk,kxyz->mxyz', select, kl_blocks.astype(jnp.float32))
    deps = region_gain[region_labels][None] * summed
    heights = jnp.arange(NZ, dtype=jnp.int32)
    profile = jnp.where(heights[None, None, :] == source_z[:, :, None], source_amp[:, :, None], 0.0).astype(jnp.float32)
    zeros_field = jnp.zeros_like(profile)
    efield, hfield = (e_init, h_init)
    tan_e = jnp.zeros((MODES,) + e_init.shape, jnp.float32)
    tan_h = jnp.zeros((MODES,) + e_init.shape, jnp.float32)
    deps_col = deps[:, None]
    for number in range(STEPS):
        wave = math.cos(OMEGA_FREQ * (number + 0.5) * DT_STEP)
        hfield = hfield - DT_STEP * curl_forward(pad_wrap(efield))
        tan_h = tan_h - DT_STEP * curl_forward(pad_wrap(tan_e))
        current = jnp.stack([zeros_field, zeros_field, profile * wave])
        drive = curl_backward(pad_wrap(hfield)) + current
        efield = efield + DT_STEP * inv_eps * drive
        tan_e = tan_e + DT_STEP * inv_eps * curl_backward(pad_wrap(tan_h)) - DT_STEP * deps_col * inv_eps * inv_eps * drive[None]
    return (tan_e, tan_h)
```

```python
import functools
import math

import jax
import jax.numpy as jnp
from jax import lax
from jax.experimental import pallas as pl
from jax.experimental.pallas import tpu as pltpu
from jax.sharding import PartitionSpec as P

STEPS = 10
DT_STEP = 0.99 / math.sqrt(3.0)
OMEGA_FREQ = 0.7

GROUP = 4
TILE = 8
FULL = 32000.0
FINE = 256.0
F32 = jnp.float32
VMEM_LIMIT = 48 * 1024 * 1024


def iota(axis, rows=TILE):
    return lax.broadcasted_iota(jnp.int32, (rows, 128), axis)


def scale_code(largest):
    return jnp.clip(jnp.ceil(jnp.log2(largest) * FINE) + 1.0, -FULL, FULL)


def to_codes(values, code):
    return jnp.round(values * (jnp.exp2(code * (-1.0 / FINE)) * FULL))


def scale_of(code):
    return jnp.exp2(code * (1.0 / FINE)) * (1.0 / FULL)


def narrow(tiles):
    return jnp.concatenate(tiles, 0).astype(jnp.int32).astype(jnp.int16)


def wide(codes):
    return codes.astype(jnp.int32).astype(F32)


def lane(tile, at):
    return jnp.broadcast_to(tile[:, at : at + 1], tile.shape)


def pack_kernel(
    size, me, modes, e, h, labels, kl, source_z, source_amp,
    packed, own, own_part, *rest,
):
    nx, ny = size
    parts, (label_rows, z_rows, amp_rows) = rest[:-3], rest[-3:]
    ratio, plane, stride = nx // GROUP, nx * ny, nx // GROUP * ny
    label_rows[:plane] = labels[...].astype(F32)
    label_rows[plane:] = jnp.zeros((plane, 128), F32)
    z_rows[...] = jnp.zeros(z_rows.shape, F32)
    amp_rows[...] = jnp.zeros(amp_rows.shape, F32)
    z_rows[nx:, :ny] = source_z[...].astype(F32)
    amp_rows[nx:, :ny] = source_amp[...]
    low, lanes = iota(0) < GROUP, iota(1)

    blocks = kl.shape[0] // plane
    rows16 = iota(0, 16)
    weights = [
        [(modes[me[0] * blocks + j] == (me[0] ^ d)).astype(F32) for j in range(blocks)]
        for d in range(len(parts) + 1)
    ]
    codes = [jnp.zeros((16, 128), F32) for _ in parts]
    for k in range(plane // 16):
        tiles = [kl[j * plane + 16 * k : j * plane + 16 * k + 16].astype(F32) for j in range(blocks)]
        for d in range(len(parts) + 1):
            total = sum(weights[d][j] * tiles[j] for j in range(blocks))
            if d == 0:
                own_part[16 * k : 16 * k + 16] = total
                continue
            halves = []
            for i in range(2):
                half = total[TILE * i : TILE * i + TILE]
                code = scale_code(jnp.max(jnp.abs(half), axis=(0, 1), keepdims=True))
                halves.append(to_codes(half, code))
                codes[d - 1] = jnp.where(rows16 == 2 * k + i, code, codes[d - 1])
            parts[d - 1][16 * k : 16 * k + 16] = narrow(halves)
    for d, part in enumerate(parts):
        part[plane:] = narrow([codes[d]])

    for y in range(ny):
        for r in range(ratio):
            at = r * ny + y
            tiles = [e[pl.ds(at, TILE, stride=stride)], h[pl.ds(at, TILE, stride=stride)]]
            e_last = e[pl.ds(at + plane, TILE, stride=stride)]
            h_last = h[pl.ds(at + plane, TILE, stride=stride)]
            tiles.append(jnp.where(low, pltpu.roll(e_last, GROUP, 0), h_last))
            label = label_rows[pl.ds(at, TILE, stride=stride)]
            height = lane(z_rows[pl.ds(r, TILE, stride=ratio)], y)
            amp = lane(amp_rows[pl.ds(r, TILE, stride=ratio)], y)
            coded, meta = [], jnp.zeros((TILE, 128), F32)
            for i, tile in enumerate(tiles):
                code = scale_code(jnp.broadcast_to(jnp.max(jnp.abs(tile), axis=1, keepdims=True), tile.shape))
                coded.append(to_codes(tile, code))
                meta = jnp.where(lanes == 2 * i, pltpu.roll(code, GROUP, 0), meta)
                meta = jnp.where(lanes == 2 * i + 1, code, meta)
            meta = jnp.where(lanes == 6, height, meta)
            amp_code = scale_code(jnp.abs(amp))
            meta = jnp.where(lanes == 7, to_codes(amp, amp_code), meta)
            meta = jnp.where(lanes == 8, amp_code, meta)
            own_meta = jnp.where(lanes == 6, height, jnp.where(lanes == 7, amp, 0.0))
            coded.append(jnp.where(low, label, meta))
            tiles.append(jnp.where(low, label, own_meta))
            base = (y * ratio + r) * 32
            packed[base : base + 16] = narrow(coded[:2])
            packed[base + 16 : base + 32] = narrow(coded[2:])
            for i, tile in enumerate(tiles):
                own[base + TILE * i : base + TILE * i + TILE] = tile


def sum_kernel(size, own_part, *rest):
    nx, ny = size
    parts, (packed, own, total) = rest[:-3], rest[-3:]
    ratio, plane, stride = nx // GROUP, nx * ny, nx // GROUP * ny
    scales = [scale_of(wide(part[plane : plane + 16])) for part in parts]
    total[:plane] = jnp.zeros((plane, 128), F32)
    total[2 * plane :] = jnp.zeros((plane, 128), F32)
    for k in range(plane // 16):
        coded = [wide(part[16 * k : 16 * k + 16]) for part in parts]
        for i in range(2):
            at = 16 * k + TILE * i
            tile = own_part[at : at + TILE]
            for c, s in zip(coded, scales):
                tile = tile + c[TILE * i : TILE * i + TILE] * s[2 * k + i : 2 * k + i + 1]
            total[plane + at : plane + at + TILE] = tile
    low, rows16 = iota(0) < GROUP, iota(0, 16)
    codes = jnp.zeros((16, 128), F32)
    held = []
    for pair in range(ny // 2):
        for r in range(ratio):
            at = r * ny + 2 * pair
            even = total[pl.ds(plane + at, TILE, stride=stride)]
            odd = total[pl.ds(at + 1, TILE, stride=stride)]
            tile = jnp.where(low, even, odd)
            unit = pair * ratio + r
            own[TILE * unit : TILE * unit + TILE] = tile
            code = scale_code(jnp.max(jnp.abs(tile), axis=(0, 1), keepdims=True))
            codes = jnp.where(rows16 == unit, code, codes)
            held.append(to_codes(tile, code))
            if len(held) == 2:
                packed[TILE * (unit - 1) : TILE * (unit + 1)] = narrow(held)
                held = []
    packed[plane:] = narrow([codes])


def x_up(tiles):
    rows = tiles[0].shape[0]
    return tiles[1:] + [pltpu.roll(tiles[0], rows - 1, 0)]


def x_down(tiles):
    return [pltpu.roll(tiles[-1], 1, 0)] + tiles[:-1]


def z_up(tiles):
    last = iota(1, tiles[0].shape[0]) == 127
    return [jnp.where(last, 0.0, pltpu.roll(t, 127, 1)) for t in tiles]


def z_down(tiles):
    first = iota(1, tiles[0].shape[0]) == 0
    return [jnp.where(first, 0.0, pltpu.roll(t, 1, 1)) for t in tiles]


def add_curl_forward(magnetic, now, above):
    ex, ey, ez = now
    above_x, _, above_z = above
    ups = (z_up(ex), z_up(ey), x_up(ey), x_up(ez))
    out = [[], [], []]
    for r in range(len(ex)):
        curl = (
            (above_z[r] - ez[r]) - (ups[1][r] - ey[r]),
            (ups[0][r] - ex[r]) - (ups[3][r] - ez[r]),
            (ups[2][r] - ey[r]) - (above_x[r] - ex[r]),
        )
        for c in range(3):
            out[c].append(-curl[c] if magnetic is None else magnetic[c][r] - curl[c])
    return out


def curl_backward(now, below_x, below_z):
    hx, hy, hz = now
    downs = (z_down(hx), z_down(hy), x_down(hy), x_down(hz))
    out = [[], [], []]
    for r in range(len(hx)):
        out[0].append((hz[r] - below_z[r]) - (hy[r] - downs[1][r]))
        out[1].append((hx[r] - downs[0][r]) - (hz[r] - downs[3][r]))
        out[2].append((hy[r] - downs[2][r]) - (hx[r] - below_x[r]))
    return out


def load_row(ref, at, ratio):
    return [[ref[at, c * ratio + r] for r in range(ratio)] for c in range(3)]


def store_row(ref, at, row):
    ratio = len(row[0])
    for c in range(3):
        for r in range(ratio):
            ref[at, c * ratio + r] = row[c][r]


def flat(row):
    return [t for tiles in row for t in tiles]


def rows_of(step, ny):
    return step + 1, ny + 2 * STEPS - 1 - step


def sweep(first, end, carry, body):
    assert (end - first) % 2 == 0

    def two(i, held):
        at = first + 2 * i
        return body(at + 1, body(at, held))

    return lax.fori_loop(0, (end - first) // 2, two, carry)


def places(parity, ny):
    upper, lower = STEPS + ny, STEPS - ny
    one = jnp.where(parity == 0, upper, lower)
    three = jnp.where(parity == 0, lower, upper)
    over = STEPS - ny
    return (
        ((0, ny, STEPS),),
        ((0, ny, one),),
        ((ny - over, over, 0), (0, over, STEPS + 2 * ny)),
        ((0, ny, three),),
    )


def halves(pairs, low):
    one, two = pairs
    return [
        jnp.where(low, one, pltpu.roll(two, GROUP, 0)),
        jnp.where(low, pltpu.roll(one, GROUP, 0), two),
    ]


def base_kernel(size, order, parity, levels, gains, own, *rest):
    nx, ny = size
    ratio = nx // GROUP
    blocks, (coef, gain_out, moves, electric, magnetic, profile) = rest[:-6], rest[-6:]
    blocks = (own,) + blocks
    low, lanes = iota(0) < GROUP, iota(1)

    def pick(label, table):
        return jnp.where(label < 0.5, table[0], jnp.where(label < 1.5, table[1], table[2]))

    def unpack(y_block, y, to):
        for r in range(ratio):
            base = pl.multiple_of((y * ratio + r) * 32, 32)
            outs = []
            for first in range(0, len(order), 2):
                pair, owned = [], []
                for x_block in order[first : first + 2]:
                    ref = blocks[4 * x_block + y_block]
                    owned.append(x_block == 0 and y_block == 0)
                    if owned[-1]:
                        pair.append([ref[pl.ds(base + TILE * i, TILE)] for i in range(4)])
                    else:
                        both = [wide(ref[pl.ds(base + 16 * i, 16)]) for i in range(2)]
                        pair.append([b[TILE * i : TILE * i + TILE] for b in both for i in range(2)])
                planes = [p for i in range(4) for p in halves((pair[0][i], pair[1][i]), low)]
                meta = planes[7]
                scale = scale_of(meta)
                mine = low if owned[0] else jnp.logical_not(low)

                def scaled(value, at):
                    factor = lane(scale, at)
                    return value * (jnp.where(mine, 1.0, factor) if any(owned) else factor)

                fields = [scaled(planes[i], i) for i in range(6)]
                amp = scaled(lane(meta, 7), 8)
                inv_eps = 1.0 / pick(planes[6], levels)
                outs.append(
                    [fields[i] * DT_STEP for i in (0, 1, 4)]
                    + [fields[i] for i in (2, 3, 5)]
                    + [
                        DT_STEP * DT_STEP * inv_eps,
                        pick(planes[6], gains) * inv_eps,
                        jnp.where(lanes.astype(F32) == lane(meta, 6), amp, 0.0),
                    ]
                )
            for i in range(9):
                tile = jnp.concatenate([o[i] for o in outs], 0) if len(outs) > 1 else outs[0][i]
                if i < 3:
                    electric[to, i * ratio + r] = tile
                elif i < 6:
                    magnetic[to, (i - 3) * ratio + r] = tile
                else:
                    (coef, gain_out, profile)[i - 6][to, r] = tile

    for y_block, pieces in enumerate(places(parity[0], ny)):
        for first, count, to in pieces:

            def some(j, _, y_block=y_block, first=first, to=to):
                unpack(y_block, first + j, to + j)
                return 0

            lax.fori_loop(0, count, some, 0)

    moved = 0
    for step in range(STEPS):
        wave = math.cos(OMEGA_FREQ * (step + 0.5) * DT_STEP)
        first, end = rows_of(step, ny)
        now = load_row(electric, first - 1, ratio)
        above = load_row(electric, first, ratio)
        new = add_curl_forward(load_row(magnetic, first - 1, ratio), now, above)

        def row(at, held, step=step, wave=wave, shift=moved - first):
            now, below_x, below_z = held
            above = load_row(electric, at + 1, ratio)
            new = add_curl_forward(load_row(magnetic, at, ratio), now, above)
            if step < STEPS - 1:
                store_row(magnetic, at, new)
            drive = curl_backward(new, below_x, below_z)
            drive[2] = [d + wave * profile[at, r] for r, d in enumerate(drive[2])]
            change = [[coef[at, r] * drive[c][r] for r in range(ratio)] for c in range(3)]
            store_row(moves, at + shift, change)
            if step < STEPS - 1:
                store_row(electric, at, [[a + b for a, b in zip(now[c], change[c])] for c in range(3)])
            return above, new[0], new[2]

        sweep(first, end, (above, new[0], new[2]), row)
        moved += end - first


def tangent_kernel(size, order, parity, coef, gain, moves, own, *rest):
    nx, ny = size
    ratio, plane = nx // GROUP, nx * ny
    n_blocks = 4 * len(set(order)) - 1
    blocks, rest = (own,) + rest[:n_blocks], rest[n_blocks:]
    out_e, out_h, electric, magnetic, weight, moves_in, sems = rest
    low = iota(0) < GROUP

    copies, moved = [], 0
    for step in range(STEPS):
        first, end = rows_of(step, ny)
        there = pl.ds(moved, end - first)
        copies.append(pltpu.make_async_copy(moves.at[there], moves_in.at[there], sems.at[step]))
        moved += end - first
    for copy in copies:
        copy.start()

    scales = [None if i == 0 else scale_of(wide(b[plane : plane + 16])) for i, b in enumerate(blocks)]

    def unpack(y_block, pair, to, wanted):
        loaded = {}
        for x_block in order:
            i = 4 * x_block + y_block
            if x_block in loaded:
                continue
            tiles = []
            for r in range(ratio):
                unit = pair * ratio + r
                if i == 0:
                    tiles.append(own[TILE * unit : TILE * unit + TILE])
                else:
                    at = TILE * unit // 16 * 16
                    both = wide(blocks[i][at : at + 16])
                    half = TILE * unit - at
                    tiles.append(both[half : half + TILE] * scales[i][unit : unit + 1])
            loaded[x_block] = tiles
        for r in range(ratio):
            outs = [
                halves((loaded[order[k]][r], loaded[order[k + 1]][r]), low)
                for k in range(0, len(order), 2)
            ]
            for i in wanted:
                tile = jnp.concatenate([o[i] for o in outs], 0) if len(outs) > 1 else outs[0][i]
                weight[to + i, r] = tile * gain[to + i, r]

    for y_block, pieces in enumerate(places(parity[0], ny)):
        for first, count, to in pieces:
            for j in range(0, count, 2):
                unpack(y_block, (first + j) // 2, to + j, (0, 1))

    moved = 0
    for step in range(STEPS):
        first, end = rows_of(step, ny)
        copies[step].wait()
        shift = moved - first
        if step == 0:

            def start(at, held, shift=shift):
                change = load_row(moves_in, at + shift, ratio)
                store_row(electric, at, [[-(weight[at, r] * change[c][r]) for r in range(ratio)] for c in range(3)])
                return held

            sweep(first, end, 0, start)
        else:

            def old(at, step=step):
                return load_row(magnetic, at, ratio) if step > 1 else None

            now = load_row(electric, first - 1, ratio)
            above = load_row(electric, first, ratio)
            new = add_curl_forward(old(first - 1), now, above)

            def row(at, held, old=old, shift=shift):
                now, below_x, below_z = held
                above = load_row(electric, at + 1, ratio)
                new = add_curl_forward(old(at), now, above)
                store_row(magnetic, at, new)
                curl = curl_backward(new, below_x, below_z)
                change = load_row(moves_in, at + shift, ratio)
                store_row(
                    electric, at,
                    [[now[c][r] + (coef[at, r] * curl[c][r] - weight[at, r] * change[c][r]) for r in range(ratio)] for c in range(3)],
                )
                return above, new[0], new[2]

            sweep(first, end, (above, new[0], new[2]), row)
        moved += end - first

    at_own = GROUP * order.index(0)
    stride = ratio * ny
    for y in range(ny):
        for r in range(ratio):
            for out, ref, factor in ((out_e, electric, 1.0 / DT_STEP), (out_h, magnetic, None)):
                for c in range(3):
                    tile = ref[STEPS + y, c * ratio + r, at_own : at_own + GROUP]
                    out[pl.ds(c * plane + r * ny + y, GROUP, stride=stride)] = tile if factor is None else tile * factor


def call(kernel, name, outs, specs, scratch, flops, args, size_bytes):
    return pl.pallas_call(
        kernel,
        out_shape=outs,
        in_specs=specs,
        out_specs=tuple(pl.BlockSpec(memory_space=pltpu.VMEM) for _ in outs),
        scratch_shapes=scratch,
        compiler_params=pltpu.CompilerParams(vmem_limit_bytes=VMEM_LIMIT),
        cost_estimate=pl.CostEstimate(flops=flops, bytes_accessed=size_bytes, transcendentals=0),
        name=name,
    )(*args)


def body(sizes, e_init, h_init, eps_levels, region_gain, region_labels, kl_blocks, kl_modes, source_z, source_amp):
    n_gx, n_gy, n_mode = sizes
    _, nx, ny, nz = e_init.shape
    assert n_gy == 4 and nx % GROUP == 0 and nx >= STEPS and ny < STEPS < 2 * ny
    ratio, plane = nx // GROUP, nx * ny
    size = (nx, ny)
    vmem, smem, anywhere = (pl.BlockSpec(memory_space=s) for s in (pltpu.VMEM, pltpu.SMEM, pl.ANY))
    f32 = lambda *shape: jax.ShapeDtypeStruct(shape, F32)
    i16 = lambda *shape: jax.ShapeDtypeStruct(shape, jnp.int16)

    def over_xy(block, dx, flip):
        route = [
            (gx * n_gy + gy, (gx + dx) % n_gx * n_gy + (gy ^ flip))
            for gx in range(n_gx)
            for gy in range(n_gy)
        ]
        return lax.ppermute(block, ("gx", "gy"), route)

    def over_mode(block, flip):
        return lax.ppermute(block, "mode", [(i, i ^ flip) for i in range(n_mode)])

    me = lax.axis_index("mode").astype(jnp.int32).reshape(1)
    parity = (lax.axis_index("gy") % 2).astype(jnp.int32).reshape(1)
    packed, own, own_part, *parts = call(
        functools.partial(pack_kernel, size), "pack",
        (i16(ny * ratio * 32, nz), f32(ny * ratio * 32, nz), f32(plane, nz)) + (i16(plane + 16, nz),) * (n_mode - 1),
        [smem, smem] + [vmem] * 6,
        [pltpu.VMEM((2 * plane, nz), F32), pltpu.VMEM((2 * nx, 128), F32), pltpu.VMEM((2 * nx, 128), F32)],
        10**6,
        (
            me, kl_modes, e_init.reshape(-1, nz), h_init.reshape(-1, nz), region_labels.reshape(-1, nz),
            kl_blocks.reshape(-1, nz), source_z, source_amp,
        ),
        10**6,
    )

    moves_x = [0, -1] if n_gx == 2 else [0, -1, 1]
    order = (0, 1) if n_gx == 2 else (2, 0, 1, 1)
    groups = GROUP * len(order)

    def gather(block):
        near = [block] + [over_xy(block, dx, 0) for dx in moves_x[1:]]
        far = [over_xy(block, dx, 2) for dx in moves_x]
        return near, far

    near, far = gather(packed)
    parts = [over_mode(part, d + 1) for d, part in enumerate(parts)]

    def with_core(near, far):
        got = near[1:] + far
        sent = over_xy(jnp.concatenate(got, 0), 0, 1)
        rows = got[0].shape[0]
        first = over_xy(near[0], 0, 1)
        other = [first] + [sent[rows * i : rows * i + rows] for i in range(len(got))]
        other_near, other_far = other[: len(near)], other[len(near) :]
        return [b for four in zip(near, other_near, far, other_far) for b in four]

    deps_packed, deps_own = call(
        functools.partial(sum_kernel, size), "sum",
        (i16(plane + 16, nz), f32(plane, nz)), [vmem] * n_mode, [pltpu.VMEM((3 * plane, nz), F32)],
        10**5, (own_part, *parts), 10**5,
    )
    blocks = with_core(near, far)
    rows = ny + 2 * STEPS
    moved = sum(rows_of(step, ny)[1] - rows_of(step, ny)[0] for step in range(STEPS))
    coef, gain, moves = call(
        functools.partial(base_kernel, size, order), "base",
        (f32(rows, ratio, groups, nz), f32(rows, ratio, groups, nz), f32(moved, 3 * ratio, groups, nz)),
        [smem] * 3 + [vmem] * len(blocks),
        [pltpu.VMEM((rows, 3 * ratio, groups, nz), F32)] * 2 + [pltpu.VMEM((rows, ratio, groups, nz), F32)],
        10**7, (parity, eps_levels, region_gain, own, *blocks[1:]), 10**7,
    )
    deps = with_core(*gather(deps_packed))
    out_e, out_h = call(
        functools.partial(tangent_kernel, size, order), "tangent",
        (f32(3 * plane, nz), f32(3 * plane, nz)),
        [smem, vmem, vmem, anywhere] + [vmem] * len(deps),
        [pltpu.VMEM((rows, 3 * ratio, groups, nz), F32)] * 2
        + [
            pltpu.VMEM((rows, ratio, groups, nz), F32),
            pltpu.VMEM((moved, 3 * ratio, groups, nz), F32),
            pltpu.SemaphoreType.DMA((STEPS,)),
        ],
        10**7, (parity, coef, gain, moves, deps_own, *deps[1:]), 10**7,
    )
    shape = (1, 3, nx, ny, nz)
    return out_e.reshape(shape), out_h.reshape(shape)


def solution(mesh):
    placed = (
        P(None, "gx", "gy", None),
        P(None, "gx", "gy", None),
        P(),
        P(),
        P("gx", "gy", None),
        P("mode", "gx", "gy", None),
        P(),
        P("gx", "gy"),
        P("gx", "gy"),
    )
    return jax.shard_map(
        functools.partial(body, tuple(mesh.shape[a] for a in ("gx", "gy", "mode"))),
        mesh=mesh,
        in_specs=placed,
        out_specs=(P("mode", None, "gx", "gy", None), P("mode", None, "gx", "gy", None)),
        check_vma=False,
    )
```

```python
import functools
import math

import jax
import jax.numpy as jnp
from jax import lax
from jax.experimental import pallas as pl
from jax.experimental.pallas import tpu as pltpu
from jax.sharding import PartitionSpec as P

STEPS = 10
DT_STEP = 0.99 / math.sqrt(3.0)
OMEGA_FREQ = 0.7

GROUP = 4
TILE = 8
FULL = 32000.0
FINE = 256.0
CHUNK = 13
F32 = jnp.float32
VMEM_LIMIT = 24 * 1024 * 1024


def iota(axis, rows=TILE):
    return lax.broadcasted_iota(jnp.int32, (rows, 128), axis)


def scale_code(largest):
    return jnp.clip(jnp.ceil(jnp.log2(largest) * FINE) + 1.0, -FULL, FULL)


def to_codes(values, code):
    return jnp.round(values * (jnp.exp2(code * (-1.0 / FINE)) * FULL))


def scale_of(code):
    return jnp.exp2(code * (1.0 / FINE)) * (1.0 / FULL)


def narrow(tiles):
    return jnp.concatenate(tiles, 0).astype(jnp.int32).astype(jnp.int16)


def wide(codes):
    return codes.astype(jnp.int32).astype(F32)


def lane(tile, at):
    return jnp.broadcast_to(tile[:, at : at + 1], tile.shape)


def pack_kernel(
    size, me, modes_at, levels_at, gains_at, e_at, h_at, labels_at, kl_at, z_at, amp_at,
    packed, own, own_part, tables, *rest,
):
    nx, ny = size
    parts, rest = rest[:-11], rest[-11:]
    modes, levels, gains, e, h, labels, kl, source_z, source_amp, label_rows, sems = rest
    ratio, plane, stride = nx // GROUP, nx * ny, nx // GROUP * ny
    ends = zip(
        (modes_at, levels_at, gains_at, kl_at, e_at, h_at, labels_at, z_at, amp_at),
        (modes, levels, gains, kl, e, h, labels, source_z, source_amp),
    )
    copies = [pltpu.make_async_copy(there, here, sems.at[i]) for i, (there, here) in enumerate(ends)]
    for copy in copies:
        copy.start()
    label_rows[plane:] = jnp.zeros((plane, 128), F32)
    for copy in copies:
        copy.wait()
    label_rows[:plane] = labels[...].astype(F32)
    for i in range(3):
        at = slice(i, i + 1)
        tables[at] = jnp.full((1, 128), DT_STEP * DT_STEP) / jnp.full((1, 128), levels[i])
        tables[slice(i + 3, i + 4)] = jnp.full((1, 128), gains[i]) / jnp.full((1, 128), levels[i])
    tables[6:8] = jnp.zeros((2, 128), F32)
    heights_of = source_z[...].astype(F32)
    amps_of = source_amp[...]
    wide_lanes = lax.broadcasted_iota(jnp.int32, (TILE, nx), 1)
    turned = lax.broadcasted_iota(jnp.int32, (TILE, nx), 0)

    def column(values, y, r):
        wanted = wide_lanes == (turned - GROUP) * ratio + r
        picked = jnp.where(wanted, jnp.broadcast_to(values[y : y + 1], wanted.shape), 0.0)
        return jnp.broadcast_to(jnp.sum(picked, axis=1, keepdims=True), (TILE, 128))

    low, lanes = iota(0) < GROUP, iota(1)

    blocks = kl.shape[0] // plane
    rows16 = iota(0, 16)
    weights = [
        [(modes[me[0] * blocks + j] == (me[0] ^ d)).astype(F32) for j in range(blocks)]
        for d in range(len(parts) + 1)
    ]
    codes = [jnp.zeros((16, 128), F32) for _ in parts]
    for k in range(plane // 16):
        tiles = [kl[j * plane + 16 * k : j * plane + 16 * k + 16].astype(F32) for j in range(blocks)]
        for d in range(len(parts) + 1):
            total = sum(weights[d][j] * tiles[j] for j in range(blocks))
            if d == 0:
                own_part[16 * k : 16 * k + 16] = total
                continue
            halves = []
            for i in range(2):
                half = total[TILE * i : TILE * i + TILE]
                code = scale_code(jnp.max(jnp.abs(half), axis=(0, 1), keepdims=True))
                halves.append(to_codes(half, code))
                codes[d - 1] = jnp.where(rows16 == 2 * k + i, code, codes[d - 1])
            parts[d - 1][16 * k : 16 * k + 16] = narrow(halves)
    for d, part in enumerate(parts):
        part[plane:] = narrow([codes[d]])

    for y in range(ny):
        for r in range(ratio):
            at = r * ny + y
            tiles = [e[pl.ds(at, TILE, stride=stride)], h[pl.ds(at, TILE, stride=stride)]]
            e_last = e[pl.ds(at + plane, TILE, stride=stride)]
            h_last = h[pl.ds(at + plane, TILE, stride=stride)]
            tiles.append(jnp.where(low, pltpu.roll(e_last, GROUP, 0), h_last))
            label = label_rows[pl.ds(at, TILE, stride=stride)]
            height, amp = column(heights_of, y, r), column(amps_of, y, r)
            coded, meta = [], jnp.zeros((TILE, 128), F32)
            for i, tile in enumerate(tiles):
                code = scale_code(jnp.broadcast_to(jnp.max(jnp.abs(tile), axis=1, keepdims=True), tile.shape))
                coded.append(to_codes(tile, code))
                meta = jnp.where(lanes == 2 * i, pltpu.roll(code, GROUP, 0), meta)
                meta = jnp.where(lanes == 2 * i + 1, code, meta)
            meta = jnp.where(lanes == 6, height, meta)
            amp_code = scale_code(jnp.abs(amp))
            meta = jnp.where(lanes == 7, to_codes(amp, amp_code), meta)
            meta = jnp.where(lanes == 8, amp_code, meta)
            own_meta = jnp.where(lanes == 6, height, jnp.where(lanes == 7, amp, 0.0))
            coded.append(jnp.where(low, label, meta))
            tiles.append(jnp.where(low, label, own_meta))
            base = (y * ratio + r) * 32
            packed[base : base + 16] = narrow(coded[:2])
            packed[base + 16 : base + 32] = narrow(coded[2:])
            for i, tile in enumerate(tiles):
                own[base + TILE * i : base + TILE * i + TILE] = tile


def sum_kernel(size, own_part, *rest):
    nx, ny = size
    parts, (packed, own, total) = rest[:-3], rest[-3:]
    ratio, plane, stride = nx // GROUP, nx * ny, nx // GROUP * ny
    scales = [scale_of(wide(part[plane : plane + 16])) for part in parts]
    total[:plane] = jnp.zeros((plane, 128), F32)
    total[2 * plane :] = jnp.zeros((plane, 128), F32)
    for k in range(plane // 16):
        coded = [wide(part[16 * k : 16 * k + 16]) for part in parts]
        for i in range(2):
            at = 16 * k + TILE * i
            tile = own_part[at : at + TILE]
            for c, s in zip(coded, scales):
                tile = tile + c[TILE * i : TILE * i + TILE] * s[2 * k + i : 2 * k + i + 1]
            total[plane + at : plane + at + TILE] = tile
    low, rows16 = iota(0) < GROUP, iota(0, 16)
    codes = jnp.zeros((16, 128), F32)
    held = []
    for pair in range(ny // 2):
        for r in range(ratio):
            at = r * ny + 2 * pair
            even = total[pl.ds(plane + at, TILE, stride=stride)]
            odd = total[pl.ds(at + 1, TILE, stride=stride)]
            tile = jnp.where(low, even, odd)
            unit = pair * ratio + r
            own[TILE * unit : TILE * unit + TILE] = tile
            code = scale_code(jnp.max(jnp.abs(tile), axis=(0, 1), keepdims=True))
            codes = jnp.where(rows16 == unit, code, codes)
            held.append(to_codes(tile, code))
            if len(held) == 2:
                packed[TILE * (unit - 1) : TILE * (unit + 1)] = narrow(held)
                held = []
    packed[plane:] = narrow([codes])


def x_up(tiles):
    rows = tiles[0].shape[0]
    return tiles[1:] + [pltpu.roll(tiles[0], rows - 1, 0)]


def x_down(tiles):
    return [pltpu.roll(tiles[-1], 1, 0)] + tiles[:-1]


def z_up(tiles):
    last = iota(1, tiles[0].shape[0]) == 127
    return [jnp.where(last, 0.0, pltpu.roll(t, 127, 1)) for t in tiles]


def z_down(tiles):
    first = iota(1, tiles[0].shape[0]) == 0
    return [jnp.where(first, 0.0, pltpu.roll(t, 1, 1)) for t in tiles]


def add_curl_forward(magnetic, now, above):
    ex, ey, ez = now
    above_x, _, above_z = above
    ups = (z_up(ex), z_up(ey), x_up(ey), x_up(ez))
    out = [[], [], []]
    for r in range(len(ex)):
        curl = (
            (above_z[r] - ez[r]) - (ups[1][r] - ey[r]),
            (ups[0][r] - ex[r]) - (ups[3][r] - ez[r]),
            (ups[2][r] - ey[r]) - (above_x[r] - ex[r]),
        )
        for c in range(3):
            out[c].append(-curl[c] if magnetic is None else magnetic[c][r] - curl[c])
    return out


def curl_backward(now, below_x, below_z):
    hx, hy, hz = now
    downs = (z_down(hx), z_down(hy), x_down(hy), x_down(hz))
    out = [[], [], []]
    for r in range(len(hx)):
        out[0].append((hz[r] - below_z[r]) - (hy[r] - downs[1][r]))
        out[1].append((hx[r] - downs[0][r]) - (hz[r] - downs[3][r]))
        out[2].append((hy[r] - downs[2][r]) - (hx[r] - below_x[r]))
    return out


def load_row(ref, at, ratio):
    return [[ref[at, c * ratio + r] for r in range(ratio)] for c in range(3)]


def store_row(ref, at, row):
    ratio = len(row[0])
    for c in range(3):
        for r in range(ratio):
            ref[at, c * ratio + r] = row[c][r]


def flat(row):
    return [t for tiles in row for t in tiles]


def rows_of(step, ny):
    return step + 1, ny + 2 * STEPS - 1 - step


def chunks(first, end):
    count = -(-(end - first) // CHUNK)
    cuts = [first + (end - first) * i // count for i in range(count + 1)]
    return [range(*cut) for cut in zip(cuts, cuts[1:])]


def places(parity, ny):
    upper, lower = STEPS + ny, STEPS - ny
    one = jnp.where(parity == 0, upper, lower)
    three = jnp.where(parity == 0, lower, upper)
    over = STEPS - ny
    return (
        ((0, ny, STEPS),),
        ((0, ny, one),),
        ((ny - over, over, 0), (0, over, STEPS + 2 * ny)),
        ((0, ny, three),),
    )


def halves(pairs, low):
    one, two = pairs
    return [
        jnp.where(low, one, pltpu.roll(two, GROUP, 0)),
        jnp.where(low, pltpu.roll(one, GROUP, 0), two),
    ]


def base_kernel(size, order, parity, tables, own, *rest):
    nx, ny = size
    ratio = nx // GROUP
    blocks, (coef, gain_out, moves, electric, magnetic, profile) = rest[:-6], rest[-6:]
    blocks = (own,) + blocks
    low, lanes = iota(0) < GROUP, iota(1)
    table = [jnp.broadcast_to(tables[i : i + 1], (TILE, 128)) for i in range(6)]

    def pick(label, first):
        return jnp.where(label < 0.5, table[first], jnp.where(label < 1.5, table[first + 1], table[first + 2]))

    def unpack(y_block, y, to):
        for r in range(ratio):
            base = pl.multiple_of((y * ratio + r) * 32, 32)
            outs = []
            for first in range(0, len(order), 2):
                pair, owned = [], []
                for x_block in order[first : first + 2]:
                    ref = blocks[4 * x_block + y_block]
                    owned.append(x_block == 0 and y_block == 0)
                    if owned[-1]:
                        pair.append([ref[pl.ds(base + TILE * i, TILE)] for i in range(4)])
                    else:
                        both = [wide(ref[pl.ds(base + 16 * i, 16)]) for i in range(2)]
                        pair.append([b[TILE * i : TILE * i + TILE] for b in both for i in range(2)])
                planes = [p for i in range(4) for p in halves((pair[0][i], pair[1][i]), low)]
                meta = planes[7]
                scale = scale_of(meta)
                mine = low if owned[0] else jnp.logical_not(low)

                def scaled(value, at):
                    factor = lane(scale, at)
                    return value * (jnp.where(mine, 1.0, factor) if any(owned) else factor)

                fields = [scaled(planes[i], i) for i in range(6)]
                amp = scaled(lane(meta, 7), 8)
                outs.append(
                    [fields[i] * DT_STEP for i in (0, 1, 4)]
                    + [fields[i] for i in (2, 3, 5)]
                    + [
                        pick(planes[6], 0),
                        pick(planes[6], 3),
                        jnp.where(lanes.astype(F32) == lane(meta, 6), amp, 0.0),
                    ]
                )
            for i in range(9):
                tile = jnp.concatenate([o[i] for o in outs], 0) if len(outs) > 1 else outs[0][i]
                if i < 3:
                    electric[to, i * ratio + r] = tile
                elif i < 6:
                    magnetic[to, (i - 3) * ratio + r] = tile
                else:
                    (coef, gain_out, profile)[i - 6][to, r] = tile

    for y_block, pieces in enumerate(places(parity[0], ny)):
        for first, count, to in pieces:

            each = min(count, 4)

            def some(j, _, y_block=y_block, first=first, to=to, each=each):
                for i in range(each):
                    unpack(y_block, first + each * j + i, to + each * j + i)
                return 0

            lax.fori_loop(0, count // each, some, 0)

    moved = 0
    for step in range(STEPS):
        wave = math.cos(OMEGA_FREQ * (step + 0.5) * DT_STEP)
        first, end = rows_of(step, ny)
        now = load_row(electric, first - 1, ratio)
        above = load_row(electric, first, ratio)
        new = add_curl_forward(load_row(magnetic, first - 1, ratio), now, above)

        below_x, below_z = new[0], new[2]
        for run in chunks(first, end):
            field = [above] + [load_row(electric, at + 1, ratio) for at in run]
            above = field[-1]
            new = [
                add_curl_forward(load_row(magnetic, at, ratio), field[i], field[i + 1])
                for i, at in enumerate(run)
            ]
            for i, at in enumerate(run):
                drive = curl_backward(new[i], below_x, below_z)
                below_x, below_z = new[i][0], new[i][2]
                drive[2] = [d + wave * profile[at, r] for r, d in enumerate(drive[2])]
                change = [[coef[at, r] * drive[c][r] for r in range(ratio)] for c in range(3)]
                store_row(moves, at - first + moved, change)
                if step < STEPS - 1:
                    store_row(magnetic, at, new[i])
                    store_row(
                        electric, at,
                        [[p + q for p, q in zip(field[i][c], change[c])] for c in range(3)],
                    )
        moved += end - first


def tangent_kernel(size, order, parity, coef, gain, moves, own, *rest):
    nx, ny = size
    ratio, plane = nx // GROUP, nx * ny
    n_blocks = 4 * len(set(order)) - 1
    blocks, rest = (own,) + rest[:n_blocks], rest[n_blocks:]
    out_e, out_h, electric, magnetic, weight = rest
    low = iota(0) < GROUP

    scales = [None if i == 0 else scale_of(wide(b[plane : plane + 16])) for i, b in enumerate(blocks)]

    def unpack(y_block, pair, to, wanted):
        loaded = {}
        for x_block in order:
            i = 4 * x_block + y_block
            if x_block in loaded:
                continue
            tiles = []
            for r in range(ratio):
                unit = pair * ratio + r
                if i == 0:
                    tiles.append(own[TILE * unit : TILE * unit + TILE])
                else:
                    at = TILE * unit // 16 * 16
                    both = wide(blocks[i][at : at + 16])
                    half = TILE * unit - at
                    tiles.append(both[half : half + TILE] * scales[i][unit : unit + 1])
            loaded[x_block] = tiles
        for r in range(ratio):
            outs = [
                halves((loaded[order[k]][r], loaded[order[k + 1]][r]), low)
                for k in range(0, len(order), 2)
            ]
            for i in wanted:
                tile = jnp.concatenate([o[i] for o in outs], 0) if len(outs) > 1 else outs[0][i]
                weight[to + i, r] = tile * gain[to + i, r]

    for y_block, pieces in enumerate(places(parity[0], ny)):
        for first, count, to in pieces:
            for j in range(0, count, 2):
                unpack(y_block, (first + j) // 2, to + j, (0, 1))

    moved = 0
    for step in range(STEPS):
        first, end = rows_of(step, ny)
        shift = moved - first
        if step == 0:

            for at in range(first, end):
                change = load_row(moves, at + shift, ratio)
                store_row(electric, at, [[-(weight[at, r] * change[c][r]) for r in range(ratio)] for c in range(3)])
        else:

            def old(at, step=step):
                return load_row(magnetic, at, ratio) if step > 1 else None

            now = load_row(electric, first - 1, ratio)
            above = load_row(electric, first, ratio)
            new = add_curl_forward(old(first - 1), now, above)

            below_x, below_z = new[0], new[2]
            for run in chunks(first, end):
                field = [above] + [load_row(electric, at + 1, ratio) for at in run]
                above = field[-1]
                new = [add_curl_forward(old(at), field[i], field[i + 1]) for i, at in enumerate(run)]
                for i, at in enumerate(run):
                    curl = curl_backward(new[i], below_x, below_z)
                    below_x, below_z = new[i][0], new[i][2]
                    change = load_row(moves, at + shift, ratio)
                    store_row(magnetic, at, new[i])
                    store_row(
                        electric, at,
                        [
                            [
                                field[i][c][r] + (coef[at, r] * curl[c][r] - weight[at, r] * change[c][r])
                                for r in range(ratio)
                            ]
                            for c in range(3)
                        ],
                    )
        moved += end - first

    at_own = GROUP * order.index(0)
    stride = ratio * ny
    for y in range(ny):
        for r in range(ratio):
            for out, ref, factor in ((out_e, electric, 1.0 / DT_STEP), (out_h, magnetic, None)):
                for c in range(3):
                    tile = ref[STEPS + y, c * ratio + r, at_own : at_own + GROUP]
                    out[pl.ds(c * plane + r * ny + y, GROUP, stride=stride)] = tile if factor is None else tile * factor


def call(kernel, name, outs, specs, scratch, about_us, args, vmem=VMEM_LIMIT):
    return pl.pallas_call(
        kernel,
        out_shape=outs,
        in_specs=specs,
        out_specs=tuple(pl.BlockSpec(memory_space=pltpu.VMEM) for _ in outs),
        scratch_shapes=scratch,
        compiler_params=pltpu.CompilerParams(vmem_limit_bytes=vmem),
        cost_estimate=pl.CostEstimate(flops=0, bytes_accessed=int(about_us * 3.7e6), transcendentals=0),
        name=name,
    )(*args)


def body(sizes, e_init, h_init, eps_levels, region_gain, region_labels, kl_blocks, kl_modes, source_z, source_amp):
    n_gx, n_gy, n_mode = sizes
    _, nx, ny, nz = e_init.shape
    assert n_gy == 4 and nx % GROUP == 0 and nx >= STEPS and ny < STEPS < 2 * ny
    ratio, plane = nx // GROUP, nx * ny
    size = (nx, ny)
    vmem, smem, hbm = (pl.BlockSpec(memory_space=s) for s in (pltpu.VMEM, pltpu.SMEM, pltpu.HBM))
    f32 = lambda *shape: jax.ShapeDtypeStruct(shape, F32)
    i16 = lambda *shape: jax.ShapeDtypeStruct(shape, jnp.int16)

    def over_xy(block, dx, flip):
        route = [
            (gx * n_gy + gy, (gx + dx) % n_gx * n_gy + (gy ^ flip))
            for gx in range(n_gx)
            for gy in range(n_gy)
        ]
        return lax.ppermute(block, ("gx", "gy"), route)

    def over_mode(block, flip):
        return lax.ppermute(block, "mode", [(i, i ^ flip) for i in range(n_mode)])

    me = lax.axis_index("mode").astype(jnp.int32).reshape(1)
    parity = (lax.axis_index("gy") % 2).astype(jnp.int32).reshape(1)
    packed, own, own_part, tables, *parts = call(
        functools.partial(pack_kernel, size), "pack",
        (i16(ny * ratio * 32, nz), f32(ny * ratio * 32, nz), f32(plane, nz), f32(TILE, nz))
        + (i16(plane + 16, nz),) * (n_mode - 1),
        [smem] + [hbm] * 9,
        [pltpu.SMEM(a.shape, a.dtype) for a in (kl_modes, eps_levels, region_gain)]
        + [pltpu.VMEM((3 * plane, nz), F32)] * 2
        + [pltpu.VMEM((plane, nz), jnp.int32), pltpu.VMEM((kl_blocks.shape[0] * plane, nz), kl_blocks.dtype)]
        + [pltpu.VMEM((ny, nx), jnp.int32), pltpu.VMEM((ny, nx), F32), pltpu.VMEM((2 * plane, nz), F32)]
        + [pltpu.SemaphoreType.DMA((9,))],
        1.5,
        (
            me,
            *(
                pltpu.with_memory_space_constraint(a, pltpu.HBM)
                for a in (
                    kl_modes, eps_levels, region_gain, e_init.reshape(-1, nz), h_init.reshape(-1, nz),
                    region_labels.reshape(-1, nz), kl_blocks.reshape(-1, nz), source_z.T, source_amp.T,
                )
            ),
        ),
    )

    moves_x = [0, -1] if n_gx == 2 else [0, -1, 1]
    order = (0, 1) if n_gx == 2 else (2, 0, 1, 1)
    groups = GROUP * len(order)

    def gather(block):
        near = [block] + [over_xy(block, dx, 0) for dx in moves_x[1:]]
        far = [over_xy(block, dx, 2) for dx in moves_x]
        return near, far

    near, far = gather(packed)
    parts = [over_mode(part, d + 1) for d, part in enumerate(parts)]

    def with_core(near, far):
        got = near[1:] + far
        sent = over_xy(jnp.concatenate(got, 0), 0, 1)
        rows = got[0].shape[0]
        first = over_xy(near[0], 0, 1)
        other = [first] + [sent[rows * i : rows * i + rows] for i in range(len(got))]
        other_near, other_far = other[: len(near)], other[len(near) :]
        return [b for four in zip(near, other_near, far, other_far) for b in four]

    deps_packed, deps_own = call(
        functools.partial(sum_kernel, size), "sum",
        (i16(plane + 16, nz), f32(plane, nz)), [vmem] * n_mode, [pltpu.VMEM((3 * plane, nz), F32)],
        0.3, (own_part, *parts),
    )
    near, far, deps_packed = lax.optimization_barrier((near, far, deps_packed))
    blocks = with_core(near, far)
    rows = ny + 2 * STEPS
    moved = sum(rows_of(step, ny)[1] - rows_of(step, ny)[0] for step in range(STEPS))
    coef, gain, moves = call(
        functools.partial(base_kernel, size, order), "base",
        (f32(rows, ratio, groups, nz), f32(rows, ratio, groups, nz), f32(moved, 3 * ratio, groups, nz)),
        [smem] + [vmem] * (1 + len(blocks)),
        [pltpu.VMEM((rows, 3 * ratio, groups, nz), F32)] * 2 + [pltpu.VMEM((rows, ratio, groups, nz), F32)],
        5.0, (parity, tables, own, *blocks[1:]),
    )
    deps = with_core(*gather(deps_packed))
    out_e, out_h = call(
        functools.partial(tangent_kernel, size, order), "tangent",
        (f32(3 * plane, nz), f32(3 * plane, nz)),
        [smem] + [vmem] * (3 + len(deps)),
        [pltpu.VMEM((rows, 3 * ratio, groups, nz), F32)] * 2 + [pltpu.VMEM((rows, ratio, groups, nz), F32)],
        4.0, (parity, coef, gain, moves, deps_own, *deps[1:]),
    )
    shape = (1, 3, nx, ny, nz)
    return out_e.reshape(shape), out_h.reshape(shape)


def solution(mesh):
    placed = (
        P(None, "gx", "gy", None),
        P(None, "gx", "gy", None),
        P(),
        P(),
        P("gx", "gy", None),
        P("mode", "gx", "gy", None),
        P(),
        P("gx", "gy"),
        P("gx", "gy"),
    )
    return jax.shard_map(
        functools.partial(body, tuple(mesh.shape[a] for a in ("gx", "gy", "mode"))),
        mesh=mesh,
        in_specs=placed,
        out_specs=(P("mode", None, "gx", "gy", None), P("mode", None, "gx", "gy", None)),
        check_vma=False,
    )
```

```python
import functools
import math

import jax
import jax.numpy as jnp
from jax import lax
from jax.experimental import pallas as pl
from jax.experimental.pallas import tpu as pltpu
from jax.sharding import PartitionSpec as P

STEPS = 10
DT_STEP = 0.99 / math.sqrt(3.0)
OMEGA_FREQ = 0.7

GROUP = 4
TILE = 8
FULL = 32000.0
FINE = 256.0
FIRST_STEPS = 5
CHUNK = 13
F32 = jnp.float32
VMEM_LIMIT = 24 * 1024 * 1024


def iota(axis, rows=TILE):
    return lax.broadcasted_iota(jnp.int32, (rows, 128), axis)


def scale_code(largest):
    return jnp.clip(jnp.ceil(jnp.log2(largest) * FINE) + 1.0, -FULL, FULL)


def to_codes(values, code):
    return jnp.round(values * (jnp.exp2(code * (-1.0 / FINE)) * FULL))


def scale_of(code):
    return jnp.exp2(code * (1.0 / FINE)) * (1.0 / FULL)


def narrow(tiles):
    return jnp.concatenate(tiles, 0).astype(jnp.int32).astype(jnp.int16)


def wide(codes):
    return codes.astype(jnp.int32).astype(F32)


def lane(tile, at):
    return jnp.broadcast_to(tile[:, at : at + 1], tile.shape)


def pack_kernel(
    size, me, modes_at, levels_at, gains_at, e_at, h_at, labels_at, kl_at, z_at, amp_at,
    packed, own, own_part, tables, *rest,
):
    nx, ny = size
    parts, rest = rest[:-11], rest[-11:]
    modes, levels, gains, e, h, labels, kl, source_z, source_amp, label_rows, sems = rest
    ratio, plane, stride = nx // GROUP, nx * ny, nx // GROUP * ny
    ends = zip(
        (modes_at, levels_at, gains_at, kl_at, e_at, h_at, labels_at, z_at, amp_at),
        (modes, levels, gains, kl, e, h, labels, source_z, source_amp),
    )
    copies = [pltpu.make_async_copy(there, here, sems.at[i]) for i, (there, here) in enumerate(ends)]
    for copy in copies:
        copy.start()
    label_rows[plane:] = jnp.zeros((plane, 128), F32)
    for copy in copies:
        copy.wait()
    label_rows[:plane] = labels[...].astype(F32)
    for i in range(3):
        at = slice(i, i + 1)
        tables[at] = jnp.full((1, 128), DT_STEP * DT_STEP) / jnp.full((1, 128), levels[i])
        tables[slice(i + 3, i + 4)] = jnp.full((1, 128), gains[i]) / jnp.full((1, 128), levels[i])
    tables[6:8] = jnp.zeros((2, 128), F32)
    heights_of = source_z[...].astype(F32)
    amps_of = source_amp[...]
    wide_lanes = lax.broadcasted_iota(jnp.int32, (TILE, nx), 1)
    turned = lax.broadcasted_iota(jnp.int32, (TILE, nx), 0)

    def column(values, y, r):
        wanted = wide_lanes == (turned - GROUP) * ratio + r
        picked = jnp.where(wanted, jnp.broadcast_to(values[y : y + 1], wanted.shape), 0.0)
        return jnp.broadcast_to(jnp.sum(picked, axis=1, keepdims=True), (TILE, 128))

    low, lanes = iota(0) < GROUP, iota(1)

    blocks = kl.shape[0] // plane
    rows16 = iota(0, 16)
    weights = [
        [(modes[me[0] * blocks + j] == (me[0] ^ d)).astype(F32) for j in range(blocks)]
        for d in range(len(parts) + 1)
    ]
    codes = [jnp.zeros((16, 128), F32) for _ in parts]
    for k in range(plane // 16):
        tiles = [kl[j * plane + 16 * k : j * plane + 16 * k + 16].astype(F32) for j in range(blocks)]
        for d in range(len(parts) + 1):
            total = sum(weights[d][j] * tiles[j] for j in range(blocks))
            if d == 0:
                own_part[16 * k : 16 * k + 16] = total
                continue
            halves = []
            for i in range(2):
                half = total[TILE * i : TILE * i + TILE]
                code = scale_code(jnp.max(jnp.abs(half), axis=(0, 1), keepdims=True))
                halves.append(to_codes(half, code))
                codes[d - 1] = jnp.where(rows16 == 2 * k + i, code, codes[d - 1])
            parts[d - 1][16 * k : 16 * k + 16] = narrow(halves)
    for d, part in enumerate(parts):
        part[plane:] = narrow([codes[d]])

    for y in range(ny):
        for r in range(ratio):
            at = r * ny + y
            tiles = [e[pl.ds(at, TILE, stride=stride)], h[pl.ds(at, TILE, stride=stride)]]
            e_last = e[pl.ds(at + plane, TILE, stride=stride)]
            h_last = h[pl.ds(at + plane, TILE, stride=stride)]
            tiles.append(jnp.where(low, pltpu.roll(e_last, GROUP, 0), h_last))
            label = label_rows[pl.ds(at, TILE, stride=stride)]
            height, amp = column(heights_of, y, r), column(amps_of, y, r)
            coded, meta = [], jnp.zeros((TILE, 128), F32)
            for i, tile in enumerate(tiles):
                code = scale_code(jnp.broadcast_to(jnp.max(jnp.abs(tile), axis=1, keepdims=True), tile.shape))
                coded.append(to_codes(tile, code))
                meta = jnp.where(lanes == 2 * i, pltpu.roll(code, GROUP, 0), meta)
                meta = jnp.where(lanes == 2 * i + 1, code, meta)
            meta = jnp.where(lanes == 6, height, meta)
            amp_code = scale_code(jnp.abs(amp))
            meta = jnp.where(lanes == 7, to_codes(amp, amp_code), meta)
            meta = jnp.where(lanes == 8, amp_code, meta)
            own_meta = jnp.where(lanes == 6, height, jnp.where(lanes == 7, amp, 0.0))
            coded.append(jnp.where(low, label, meta))
            tiles.append(jnp.where(low, label, own_meta))
            base = (y * ratio + r) * 32
            packed[base : base + 16] = narrow(coded[:2])
            packed[base + 16 : base + 32] = narrow(coded[2:])
            for i, tile in enumerate(tiles):
                own[base + TILE * i : base + TILE * i + TILE] = tile


def sum_kernel(size, own_part, *rest):
    nx, ny = size
    parts, (packed, own, total) = rest[:-3], rest[-3:]
    ratio, plane, stride = nx // GROUP, nx * ny, nx // GROUP * ny
    scales = [scale_of(wide(part[plane : plane + 16])) for part in parts]
    total[:plane] = jnp.zeros((plane, 128), F32)
    total[2 * plane :] = jnp.zeros((plane, 128), F32)
    for k in range(plane // 16):
        coded = [wide(part[16 * k : 16 * k + 16]) for part in parts]
        for i in range(2):
            at = 16 * k + TILE * i
            tile = own_part[at : at + TILE]
            for c, s in zip(coded, scales):
                tile = tile + c[TILE * i : TILE * i + TILE] * s[2 * k + i : 2 * k + i + 1]
            total[plane + at : plane + at + TILE] = tile
    low, rows16 = iota(0) < GROUP, iota(0, 16)
    codes = jnp.zeros((16, 128), F32)
    held = []
    for pair in range(ny // 2):
        for r in range(ratio):
            at = r * ny + 2 * pair
            even = total[pl.ds(plane + at, TILE, stride=stride)]
            odd = total[pl.ds(at + 1, TILE, stride=stride)]
            tile = jnp.where(low, even, odd)
            unit = pair * ratio + r
            own[TILE * unit : TILE * unit + TILE] = tile
            code = scale_code(jnp.max(jnp.abs(tile), axis=(0, 1), keepdims=True))
            codes = jnp.where(rows16 == unit, code, codes)
            held.append(to_codes(tile, code))
            if len(held) == 2:
                packed[TILE * (unit - 1) : TILE * (unit + 1)] = narrow(held)
                held = []
    packed[plane:] = narrow([codes])


def x_up(tiles):
    rows = tiles[0].shape[0]
    return tiles[1:] + [pltpu.roll(tiles[0], rows - 1, 0)]


def x_down(tiles):
    return [pltpu.roll(tiles[-1], 1, 0)] + tiles[:-1]


def z_up(tiles):
    last = iota(1, tiles[0].shape[0]) == 127
    return [jnp.where(last, 0.0, pltpu.roll(t, 127, 1)) for t in tiles]


def z_down(tiles):
    first = iota(1, tiles[0].shape[0]) == 0
    return [jnp.where(first, 0.0, pltpu.roll(t, 1, 1)) for t in tiles]


def add_curl_forward(magnetic, now, above):
    ex, ey, ez = now
    above_x, _, above_z = above
    ups = (z_up(ex), z_up(ey), x_up(ey), x_up(ez))
    out = [[], [], []]
    for r in range(len(ex)):
        curl = (
            (above_z[r] - ez[r]) - (ups[1][r] - ey[r]),
            (ups[0][r] - ex[r]) - (ups[3][r] - ez[r]),
            (ups[2][r] - ey[r]) - (above_x[r] - ex[r]),
        )
        for c in range(3):
            out[c].append(-curl[c] if magnetic is None else magnetic[c][r] - curl[c])
    return out


def curl_backward(now, below_x, below_z):
    hx, hy, hz = now
    downs = (z_down(hx), z_down(hy), x_down(hy), x_down(hz))
    out = [[], [], []]
    for r in range(len(hx)):
        out[0].append((hz[r] - below_z[r]) - (hy[r] - downs[1][r]))
        out[1].append((hx[r] - downs[0][r]) - (hz[r] - downs[3][r]))
        out[2].append((hy[r] - downs[2][r]) - (hx[r] - below_x[r]))
    return out


def load_row(ref, at, ratio):
    return [[ref[at, c * ratio + r] for r in range(ratio)] for c in range(3)]


def store_row(ref, at, row):
    ratio = len(row[0])
    for c in range(3):
        for r in range(ratio):
            ref[at, c * ratio + r] = row[c][r]


def flat(row):
    return [t for tiles in row for t in tiles]


def rows_of(step, ny):
    return step + 1, ny + 2 * STEPS - 1 - step


def chunks(first, end):
    count = -(-(end - first) // CHUNK)
    cuts = [first + (end - first) * i // count for i in range(count + 1)]
    return [range(*cut) for cut in zip(cuts, cuts[1:])]


def places(parity, ny):
    upper, lower = STEPS + ny, STEPS - ny
    one = jnp.where(parity == 0, upper, lower)
    three = jnp.where(parity == 0, lower, upper)
    over = STEPS - ny
    return (
        ((0, ny, STEPS),),
        ((0, ny, one),),
        ((ny - over, over, 0), (0, over, STEPS + 2 * ny)),
        ((0, ny, three),),
    )


def halves(pairs, low):
    one, two = pairs
    return [
        jnp.where(low, one, pltpu.roll(two, GROUP, 0)),
        jnp.where(low, pltpu.roll(one, GROUP, 0), two),
    ]


def base_kernel(size, order, parity, tables, own, *rest):
    nx, ny = size
    ratio = nx // GROUP
    blocks, (coef, gain_out, moves, electric, magnetic, profile) = rest[:-6], rest[-6:]
    blocks = (own,) + blocks
    low, lanes = iota(0) < GROUP, iota(1)
    table = [jnp.broadcast_to(tables[i : i + 1], (TILE, 128)) for i in range(6)]

    def pick(label, first):
        return jnp.where(label < 0.5, table[first], jnp.where(label < 1.5, table[first + 1], table[first + 2]))

    def unpack(y_block, y, to):
        for r in range(ratio):
            base = pl.multiple_of((y * ratio + r) * 32, 32)
            outs = []
            for first in range(0, len(order), 2):
                pair, owned = [], []
                for x_block in order[first : first + 2]:
                    ref = blocks[4 * x_block + y_block]
                    owned.append(x_block == 0 and y_block == 0)
                    if owned[-1]:
                        pair.append([ref[pl.ds(base + TILE * i, TILE)] for i in range(4)])
                    else:
                        both = [wide(ref[pl.ds(base + 16 * i, 16)]) for i in range(2)]
                        pair.append([b[TILE * i : TILE * i + TILE] for b in both for i in range(2)])
                planes = [p for i in range(4) for p in halves((pair[0][i], pair[1][i]), low)]
                meta = planes[7]
                scale = scale_of(meta)
                mine = low if owned[0] else jnp.logical_not(low)

                def scaled(value, at):
                    factor = lane(scale, at)
                    return value * (jnp.where(mine, 1.0, factor) if any(owned) else factor)

                fields = [scaled(planes[i], i) for i in range(6)]
                amp = scaled(lane(meta, 7), 8)
                outs.append(
                    [fields[i] * DT_STEP for i in (0, 1, 4)]
                    + [fields[i] for i in (2, 3, 5)]
                    + [
                        pick(planes[6], 0),
                        pick(planes[6], 3),
                        jnp.where(lanes.astype(F32) == lane(meta, 6), amp, 0.0),
                    ]
                )
            for i in range(9):
                tile = jnp.concatenate([o[i] for o in outs], 0) if len(outs) > 1 else outs[0][i]
                if i < 3:
                    electric[to, i * ratio + r] = tile
                elif i < 6:
                    magnetic[to, (i - 3) * ratio + r] = tile
                else:
                    (coef, gain_out, profile)[i - 6][to, r] = tile

    for y_block, pieces in enumerate(places(parity[0], ny)):
        for first, count, to in pieces:

            each = min(count, 4)

            def some(j, _, y_block=y_block, first=first, to=to, each=each):
                for i in range(each):
                    unpack(y_block, first + each * j + i, to + each * j + i)
                return 0

            lax.fori_loop(0, count // each, some, 0)

    base_steps(size, range(FIRST_STEPS), coef, profile, moves, (electric, magnetic), (electric, magnetic))


def later_kernel(size, coef, profile, electric, magnetic, moves, electric_held, magnetic_held):
    base_steps(
        size, range(FIRST_STEPS, STEPS), coef, profile, moves, (electric, magnetic), (electric_held, magnetic_held)
    )


def base_steps(size, steps, coef, profile, moves, fields, held):
    nx, ny = size
    ratio = nx // GROUP
    to_electric, to_magnetic = held
    moved = 0
    for step in steps:
        electric, magnetic = fields if step == steps[0] else held
        wave = math.cos(OMEGA_FREQ * (step + 0.5) * DT_STEP)
        first, end = rows_of(step, ny)
        now = load_row(electric, first - 1, ratio)
        above = load_row(electric, first, ratio)
        new = add_curl_forward(load_row(magnetic, first - 1, ratio), now, above)
        below_x, below_z = new[0], new[2]
        for run in chunks(first, end):
            field = [above] + [load_row(electric, at + 1, ratio) for at in run]
            above = field[-1]
            new = [
                add_curl_forward(load_row(magnetic, at, ratio), field[i], field[i + 1])
                for i, at in enumerate(run)
            ]
            for i, at in enumerate(run):
                drive = curl_backward(new[i], below_x, below_z)
                below_x, below_z = new[i][0], new[i][2]
                drive[2] = [d + wave * profile[at, r] for r, d in enumerate(drive[2])]
                change = [[coef[at, r] * drive[c][r] for r in range(ratio)] for c in range(3)]
                store_row(moves, at - first + moved, change)
                if step < STEPS - 1:
                    store_row(to_magnetic, at, new[i])
                    store_row(
                        to_electric, at,
                        [[p + q for p, q in zip(field[i][c], change[c])] for c in range(3)],
                    )
        moved += end - first


def tangent_kernel(size, order, parity, coef, gain, moves_first, moves_later, own, *rest):
    nx, ny = size
    ratio, plane = nx // GROUP, nx * ny
    n_blocks = 4 * len(set(order)) - 1
    blocks, rest = (own,) + rest[:n_blocks], rest[n_blocks:]
    out_e, out_h, electric, magnetic, weight = rest
    low = iota(0) < GROUP

    scales = [None if i == 0 else scale_of(wide(b[plane : plane + 16])) for i, b in enumerate(blocks)]

    def unpack(y_block, pair, to, wanted):
        loaded = {}
        for x_block in order:
            i = 4 * x_block + y_block
            if x_block in loaded:
                continue
            tiles = []
            for r in range(ratio):
                unit = pair * ratio + r
                if i == 0:
                    tiles.append(own[TILE * unit : TILE * unit + TILE])
                else:
                    at = TILE * unit // 16 * 16
                    both = wide(blocks[i][at : at + 16])
                    half = TILE * unit - at
                    tiles.append(both[half : half + TILE] * scales[i][unit : unit + 1])
            loaded[x_block] = tiles
        for r in range(ratio):
            outs = [
                halves((loaded[order[k]][r], loaded[order[k + 1]][r]), low)
                for k in range(0, len(order), 2)
            ]
            for i in wanted:
                tile = jnp.concatenate([o[i] for o in outs], 0) if len(outs) > 1 else outs[0][i]
                weight[to + i, r] = tile * gain[to + i, r]

    for y_block, pieces in enumerate(places(parity[0], ny)):
        for first, count, to in pieces:
            for j in range(0, count, 2):
                unpack(y_block, (first + j) // 2, to + j, (0, 1))

    moved = 0
    for step in range(STEPS):
        first, end = rows_of(step, ny)
        if step == FIRST_STEPS:
            moved = 0
        moves = moves_first if step < FIRST_STEPS else moves_later
        shift = moved - first
        if step == 0:

            for at in range(first, end):
                change = load_row(moves, at + shift, ratio)
                store_row(electric, at, [[-(weight[at, r] * change[c][r]) for r in range(ratio)] for c in range(3)])
        else:

            def old(at, step=step):
                return load_row(magnetic, at, ratio) if step > 1 else None

            now = load_row(electric, first - 1, ratio)
            above = load_row(electric, first, ratio)
            new = add_curl_forward(old(first - 1), now, above)

            below_x, below_z = new[0], new[2]
            for run in chunks(first, end):
                field = [above] + [load_row(electric, at + 1, ratio) for at in run]
                above = field[-1]
                new = [add_curl_forward(old(at), field[i], field[i + 1]) for i, at in enumerate(run)]
                for i, at in enumerate(run):
                    curl = curl_backward(new[i], below_x, below_z)
                    below_x, below_z = new[i][0], new[i][2]
                    change = load_row(moves, at + shift, ratio)
                    store_row(magnetic, at, new[i])
                    store_row(
                        electric, at,
                        [
                            [
                                field[i][c][r] + (coef[at, r] * curl[c][r] - weight[at, r] * change[c][r])
                                for r in range(ratio)
                            ]
                            for c in range(3)
                        ],
                    )
        moved += end - first

    at_own = GROUP * order.index(0)
    stride = ratio * ny
    for y in range(ny):
        for r in range(ratio):
            for out, ref, factor in ((out_e, electric, 1.0 / DT_STEP), (out_h, magnetic, None)):
                for c in range(3):
                    tile = ref[STEPS + y, c * ratio + r, at_own : at_own + GROUP]
                    out[pl.ds(c * plane + r * ny + y, GROUP, stride=stride)] = tile if factor is None else tile * factor


def call(kernel, name, outs, specs, scratch, about_us, args, vmem=VMEM_LIMIT):
    return pl.pallas_call(
        kernel,
        out_shape=outs,
        in_specs=specs,
        out_specs=tuple(pl.BlockSpec(memory_space=pltpu.VMEM) for _ in outs),
        scratch_shapes=scratch,
        compiler_params=pltpu.CompilerParams(vmem_limit_bytes=vmem),
        cost_estimate=pl.CostEstimate(flops=0, bytes_accessed=int(about_us * 3.7e6), transcendentals=0),
        name=name,
    )(*args)


def body(sizes, e_init, h_init, eps_levels, region_gain, region_labels, kl_blocks, kl_modes, source_z, source_amp):
    n_gx, n_gy, n_mode = sizes
    _, nx, ny, nz = e_init.shape
    assert n_gy == 4 and nx % GROUP == 0 and nx >= STEPS and ny < STEPS < 2 * ny
    ratio, plane = nx // GROUP, nx * ny
    size = (nx, ny)
    vmem, smem, hbm = (pl.BlockSpec(memory_space=s) for s in (pltpu.VMEM, pltpu.SMEM, pltpu.HBM))
    f32 = lambda *shape: jax.ShapeDtypeStruct(shape, F32)
    i16 = lambda *shape: jax.ShapeDtypeStruct(shape, jnp.int16)

    def over_xy(block, dx, flip):
        route = [
            (gx * n_gy + gy, (gx + dx) % n_gx * n_gy + (gy ^ flip))
            for gx in range(n_gx)
            for gy in range(n_gy)
        ]
        return lax.ppermute(block, ("gx", "gy"), route)

    def over_mode(block, flip):
        return lax.ppermute(block, "mode", [(i, i ^ flip) for i in range(n_mode)])

    me = lax.axis_index("mode").astype(jnp.int32).reshape(1)
    parity = (lax.axis_index("gy") % 2).astype(jnp.int32).reshape(1)
    packed, own, own_part, tables, *parts = call(
        functools.partial(pack_kernel, size), "pack",
        (i16(ny * ratio * 32, nz), f32(ny * ratio * 32, nz), f32(plane, nz), f32(TILE, nz))
        + (i16(plane + 16, nz),) * (n_mode - 1),
        [smem] + [hbm] * 9,
        [pltpu.SMEM(a.shape, a.dtype) for a in (kl_modes, eps_levels, region_gain)]
        + [pltpu.VMEM((3 * plane, nz), F32)] * 2
        + [pltpu.VMEM((plane, nz), jnp.int32), pltpu.VMEM((kl_blocks.shape[0] * plane, nz), kl_blocks.dtype)]
        + [pltpu.VMEM((ny, nx), jnp.int32), pltpu.VMEM((ny, nx), F32), pltpu.VMEM((2 * plane, nz), F32)]
        + [pltpu.SemaphoreType.DMA((9,))],
        1.5,
        (
            me,
            *(
                pltpu.with_memory_space_constraint(a, pltpu.HBM)
                for a in (
                    kl_modes, eps_levels, region_gain, e_init.reshape(-1, nz), h_init.reshape(-1, nz),
                    region_labels.reshape(-1, nz), kl_blocks.reshape(-1, nz), source_z.T, source_amp.T,
                )
            ),
        ),
    )

    moves_x = [0, -1] if n_gx == 2 else [0, -1, 1]
    order = (0, 1) if n_gx == 2 else (2, 0, 1, 1)
    groups = GROUP * len(order)

    def gather(block):
        near = [block] + [over_xy(block, dx, 0) for dx in moves_x[1:]]
        far = [over_xy(block, dx, 2) for dx in moves_x]
        return near, far

    parts = [over_mode(parts[d], d + 1) for d in reversed(range(len(parts)))]
    near, far = gather(packed)

    def with_core(near, far):
        got = near + far
        sent = over_xy(jnp.concatenate(got, 0), 0, 1)
        rows = got[0].shape[0]
        other = [sent[rows * i : rows * i + rows] for i in range(len(got))]
        other_near, other_far = other[: len(near)], other[len(near) :]
        return [b for four in zip(near, other_near, far, other_far) for b in four]

    deps_packed, deps_own = call(
        functools.partial(sum_kernel, size), "sum",
        (i16(plane + 16, nz), f32(plane, nz)), [vmem] * n_mode, [pltpu.VMEM((3 * plane, nz), F32)],
        0.3, (own_part, *parts),
    )
    near, far, deps_packed = lax.optimization_barrier((near, far, deps_packed))
    blocks = with_core(near, far)
    rows = ny + 2 * STEPS
    counts = [rows_of(step, ny)[1] - rows_of(step, ny)[0] for step in range(STEPS)]
    moved = [sum(counts[:FIRST_STEPS]), sum(counts[FIRST_STEPS:])]
    plane_shape, field_shape = (rows, ratio, groups, nz), (rows, 3 * ratio, groups, nz)
    deps_near, deps_far = gather(deps_packed)
    coef, gain, moves_first, electric, magnetic, profile = call(
        functools.partial(base_kernel, size, order), "base",
        (f32(*plane_shape), f32(*plane_shape), f32(moved[0], *field_shape[1:]), f32(*field_shape), f32(*field_shape), f32(*plane_shape)),
        [smem] + [vmem] * (1 + len(blocks)),
        [], 3.5, (parity, tables, own, *blocks[1:]),
    )
    deps_near, deps_far, coef, gain, moves_first = lax.optimization_barrier(
        (deps_near, deps_far, coef, gain, moves_first)
    )
    deps = with_core(deps_near, deps_far)
    (moves_later,) = call(
        functools.partial(later_kernel, size), "later",
        (f32(moved[1], *field_shape[1:]),), [vmem] * 4, [pltpu.VMEM(field_shape, F32)] * 2,
        1.5, (coef, profile, electric, magnetic),
    )
    out_e, out_h = call(
        functools.partial(tangent_kernel, size, order), "tangent",
        (f32(3 * plane, nz), f32(3 * plane, nz)),
        [smem] + [vmem] * (4 + len(deps)),
        [pltpu.VMEM(field_shape, F32)] * 2 + [pltpu.VMEM(plane_shape, F32)],
        4.0, (parity, coef, gain, moves_first, moves_later, deps_own, *deps[1:]),
    )
    shape = (1, 3, nx, ny, nz)
    return out_e.reshape(shape), out_h.reshape(shape)


def solution(mesh):
    placed = (
        P(None, "gx", "gy", None),
        P(None, "gx", "gy", None),
        P(),
        P(),
        P("gx", "gy", None),
        P("mode", "gx", "gy", None),
        P(),
        P("gx", "gy"),
        P("gx", "gy"),
    )
    return jax.shard_map(
        functools.partial(body, tuple(mesh.shape[a] for a in ("gx", "gy", "mode"))),
        mesh=mesh,
        in_specs=placed,
        out_specs=(P("mode", None, "gx", "gy", None), P("mode", None, "gx", "gy", None)),
        check_vma=False,
    )
```

```python
import functools
import math

import jax
import jax.numpy as jnp
from jax import lax
from jax.experimental import pallas as pl
from jax.experimental.pallas import tpu as pltpu
from jax.sharding import PartitionSpec as P

STEPS = 10
DT_STEP = 0.99 / math.sqrt(3.0)
OMEGA_FREQ = 0.7

GROUP = 4
TILE = 8
FULL = 32000.0
FINE = 256.0
FIRST_STEPS = 4
SCALE_AT = 4 * 8
CHUNK = 13
F32 = jnp.float32
VMEM_LIMIT = 24 * 1024 * 1024


def iota(axis, rows=TILE):
    return lax.broadcasted_iota(jnp.int32, (rows, 128), axis)


def scale_code(largest):
    return jnp.clip(jnp.ceil(jnp.log2(largest) * FINE) + 1.0, -FULL, FULL)


def to_codes(values, code):
    return jnp.round(values * (jnp.exp2(code * (-1.0 / FINE)) * FULL))


def scale_of(code):
    return jnp.exp2(code * (1.0 / FINE)) * (1.0 / FULL)


def narrow(tiles):
    return jnp.concatenate(tiles, 0).astype(jnp.int32).astype(jnp.int16)


def wide(codes):
    return codes.astype(jnp.int32).astype(F32)


def lane(tile, at):
    return jnp.broadcast_to(tile[:, at : at + 1], tile.shape)


def code_tiles(total, k, codes):
    rows, coded = iota(0, 16), []
    for i in range(2):
        tile = total[TILE * i : TILE * i + TILE]
        code = scale_code(jnp.max(jnp.abs(tile), axis=(0, 1), keepdims=True))
        coded.append(to_codes(tile, code))
        codes = jnp.where(rows == 2 * k + i, code, codes)
    return narrow(coded), codes


def decoded(part, at, plane, k):
    scales = scale_of(wide(part[at + plane : at + plane + 16]))
    coded = wide(part[at + 16 * k : at + 16 * k + 16])
    return [coded[TILE * i : TILE * i + TILE] * scales[2 * k + i : 2 * k + i + 1] for i in range(2)]


def half_kernel(size, near_part, far_parts, part):
    plane = size[0] * size[1]
    codes = jnp.zeros((16, 128), F32)
    for k in range(plane // 16):
        total = near_part[16 * k : 16 * k + 16] + jnp.concatenate(decoded(far_parts, plane + 16, plane, k), 0)
        part[16 * k : 16 * k + 16], codes = code_tiles(total, k, codes)
    part[plane:] = narrow([codes])


def field_rows(size, y, r):
    nx, ny = size
    ratio = nx // GROUP
    second, third = 16 * ny * ratio, 24 * ny * ratio
    return (
        (y * ratio + r) * 16,
        second + (y // 2 * ratio + r) * 16 + y % 2 * TILE,
        third + (y // 4 * ratio + r) * 16 + y % 4 * GROUP,
    )


def info_row(size):
    nx, ny = size
    return 28 * ny * (nx // GROUP)


def pack_kernel(
    size, me, modes_at, levels_at, gains_at, e_at, h_at, labels_at, kl_at, z_at, amp_at,
    packed, own, own_part, near_part, tables, far_parts, *rest,
):
    nx, ny = size
    modes, levels, gains, e, h, labels, kl, source_z, source_amp, label_rows, sems = rest
    ratio, plane, stride = nx // GROUP, nx * ny, nx // GROUP * ny
    ends = zip(
        (modes_at, levels_at, gains_at, kl_at, e_at, h_at, labels_at, z_at, amp_at),
        (modes, levels, gains, kl, e, h, labels, source_z, source_amp),
    )
    copies = [pltpu.make_async_copy(there, here, sems.at[i]) for i, (there, here) in enumerate(ends)]
    for copy in copies:
        copy.start()
    label_rows[plane:] = jnp.zeros((plane, 128), F32)
    for copy in copies:
        copy.wait()
    label_rows[:plane] = labels[...].astype(F32)
    for i in range(3):
        at = slice(i, i + 1)
        tables[at] = jnp.full((1, 128), DT_STEP * DT_STEP) / jnp.full((1, 128), levels[i])
        tables[slice(i + 3, i + 4)] = jnp.full((1, 128), gains[i]) / jnp.full((1, 128), levels[i])
    tables[6:8] = jnp.zeros((2, 128), F32)
    heights_of = source_z[...].astype(F32)
    amps_of = source_amp[...]
    low, lanes = iota(0) < GROUP, iota(1)

    blocks = kl.shape[0] // plane
    weights = [
        [(modes[me[0] * blocks + j] == (me[0] ^ d)).astype(F32) for j in range(blocks)] for d in (0, 2, 1, 3)
    ]
    codes = [jnp.zeros((16, 128), F32) for _ in range(2)]
    for k in range(plane // 16):
        tiles = [kl[j * plane + 16 * k : j * plane + 16 * k + 16].astype(F32) for j in range(blocks)]
        for d in range(4):
            total = sum(weights[d][j] * tiles[j] for j in range(blocks))
            if d < 2:
                (own_part, near_part)[d][16 * k : 16 * k + 16] = total
            else:
                first = (plane + 16) * (d - 2) + 16 * k
                far_parts[first : first + 16], codes[d - 2] = code_tiles(total, k, codes[d - 2])
    for i in range(2):
        first = (plane + 16) * i + plane
        far_parts[first : first + 16] = narrow([codes[i]])

    info = jnp.zeros((TILE, 128), F32)
    rows = iota(0)
    for r in range(ratio):
        labels_held = []
        for y in range(ny):
            at = r * ny + y
            tiles = [e[pl.ds(at, TILE, stride=stride)], h[pl.ds(at, TILE, stride=stride)]]
            e_last = e[pl.ds(at + plane, TILE, stride=stride)]
            h_last = h[pl.ds(at + plane, TILE, stride=stride)]
            tiles.append(jnp.where(low, pltpu.roll(e_last, GROUP, 0), h_last))
            coded = []
            for i, tile in enumerate(tiles):
                code = scale_code(jnp.max(jnp.abs(tile), axis=(0, 1), keepdims=True))
                coded.append(to_codes(tile, code))
                info = jnp.where((rows == y) & (lanes == SCALE_AT + i * ratio + r), code, info)
            first, second, third = field_rows(size, y, r)
            packed[first : first + 16] = narrow(coded[:2])
            own[first : first + TILE] = tiles[0]
            own[first + TILE : first + 16] = tiles[1]
            own[second : second + TILE] = tiles[2]
            labels_held.append(label_rows[pl.ds(at, TILE, stride=stride)])
            if y % 2 == 0:
                last_even = coded[2]
                continue
            packed[second - TILE : second + TILE] = narrow([last_even, coded[2]])
            pair = jnp.where(low, labels_held[-2], pltpu.roll(labels_held[-1], GROUP, 0))
            labels_held[-2:] = [pair]
            third = third // TILE * TILE
            own[third : third + TILE] = pair
            if len(labels_held) == 2:
                packed[third - TILE : third + TILE] = narrow(labels_held)
                labels_held = []
    amp_codes = scale_code(jnp.abs(amps_of))
    sources = [heights_of, to_codes(amps_of, amp_codes), amp_codes, amps_of]
    sources = jnp.concatenate([jnp.concatenate(sources, 0), jnp.zeros((4 * ny, 128 - nx), F32)], 1)
    sources = jnp.concatenate([sources, jnp.zeros((128 - 4 * ny, 128), F32)], 0).T[:16]
    lanes16 = iota(1, 16)
    last = info_row(size)
    info = jnp.concatenate([info, jnp.zeros((TILE, 128), F32)], 0)
    packed[last : last + 16] = jnp.where(lanes16 < 3 * ny, sources, info).astype(jnp.int32).astype(jnp.int16)
    own[last : last + 16] = jnp.where(lanes16 < ny, sources, pltpu.roll(sources, 128 - 2 * ny, 1))


def sum_kernel(size, own_part, far_parts, near_part, packed, own, total):
    nx, ny = size
    ratio, plane, stride = nx // GROUP, nx * ny, nx // GROUP * ny
    total[:plane] = jnp.zeros((plane, 128), F32)
    total[2 * plane :] = jnp.zeros((plane, 128), F32)
    for k in range(plane // 16):
        both = zip(decoded(far_parts, 0, plane, k), decoded(near_part, 0, plane, k))
        for i, (far, near) in enumerate(both):
            at = 16 * k + TILE * i
            total[plane + at : plane + at + TILE] = own_part[at : at + TILE] + far + near
    low, rows16 = iota(0) < GROUP, iota(0, 16)
    codes = jnp.zeros((16, 128), F32)
    held = []
    for pair in range(ny // 2):
        for r in range(ratio):
            at = r * ny + 2 * pair
            even = total[pl.ds(plane + at, TILE, stride=stride)]
            odd = total[pl.ds(at + 1, TILE, stride=stride)]
            tile = jnp.where(low, even, odd)
            unit = pair * ratio + r
            own[TILE * unit : TILE * unit + TILE] = tile
            code = scale_code(jnp.max(jnp.abs(tile), axis=(0, 1), keepdims=True))
            codes = jnp.where(rows16 == unit, code, codes)
            held.append(to_codes(tile, code))
            if len(held) == 2:
                packed[TILE * (unit - 1) : TILE * (unit + 1)] = narrow(held)
                held = []
    packed[plane:] = narrow([codes])


def x_up(tiles):
    rows = tiles[0].shape[0]
    return tiles[1:] + [pltpu.roll(tiles[0], rows - 1, 0)]


def x_down(tiles):
    return [pltpu.roll(tiles[-1], 1, 0)] + tiles[:-1]


def z_up(tiles):
    last = iota(1, tiles[0].shape[0]) == 127
    return [jnp.where(last, 0.0, pltpu.roll(t, 127, 1)) for t in tiles]


def z_down(tiles):
    first = iota(1, tiles[0].shape[0]) == 0
    return [jnp.where(first, 0.0, pltpu.roll(t, 1, 1)) for t in tiles]


def add_curl_forward(magnetic, now, above):
    ex, ey, ez = now
    above_x, _, above_z = above
    ups = (z_up(ex), z_up(ey), x_up(ey), x_up(ez))
    out = [[], [], []]
    for r in range(len(ex)):
        curl = (
            (above_z[r] - ez[r]) - (ups[1][r] - ey[r]),
            (ups[0][r] - ex[r]) - (ups[3][r] - ez[r]),
            (ups[2][r] - ey[r]) - (above_x[r] - ex[r]),
        )
        for c in range(3):
            out[c].append(-curl[c] if magnetic is None else magnetic[c][r] - curl[c])
    return out


def curl_backward(now, below_x, below_z):
    hx, hy, hz = now
    downs = (z_down(hx), z_down(hy), x_down(hy), x_down(hz))
    out = [[], [], []]
    for r in range(len(hx)):
        out[0].append((hz[r] - below_z[r]) - (hy[r] - downs[1][r]))
        out[1].append((hx[r] - downs[0][r]) - (hz[r] - downs[3][r]))
        out[2].append((hy[r] - downs[2][r]) - (hx[r] - below_x[r]))
    return out


def load_row(ref, at, ratio):
    return [[ref[at, c * ratio + r] for r in range(ratio)] for c in range(3)]


def store_row(ref, at, row):
    ratio = len(row[0])
    for c in range(3):
        for r in range(ratio):
            ref[at, c * ratio + r] = row[c][r]


def flat(row):
    return [t for tiles in row for t in tiles]


def rows_of(step, ny):
    return step + 1, ny + 2 * STEPS - 1 - step


def chunks(first, end):
    count = -(-(end - first) // CHUNK)
    cuts = [first + (end - first) * i // count for i in range(count + 1)]
    return [range(*cut) for cut in zip(cuts, cuts[1:])]


def places(parity, ny):
    upper, lower = STEPS + ny, STEPS - ny
    one = jnp.where(parity == 0, upper, lower)
    three = jnp.where(parity == 0, lower, upper)
    over = STEPS - ny
    return (
        ((0, ny, STEPS),),
        ((0, ny, one),),
        ((ny - over, over, 0), (0, over, STEPS + 2 * ny)),
        ((0, ny, three),),
    )


def halves(pairs, low):
    one, two = pairs
    return [
        jnp.where(low, one, pltpu.roll(two, GROUP, 0)),
        jnp.where(low, pltpu.roll(one, GROUP, 0), two),
    ]


def base_kernel(size, order, parity, tables, own, *rest):
    nx, ny = size
    ratio = nx // GROUP
    blocks, rest = rest[:-8], rest[-8:]
    coef, gain_out, moves, electric, magnetic, profile, scales, sources = rest
    blocks = (own,) + blocks
    low, lanes = iota(0) < GROUP, iota(1)
    table = [jnp.broadcast_to(tables[i : i + 1], (TILE, 128)) for i in range(6)]

    def pick(label, first):
        return jnp.where(label < 0.5, table[first], jnp.where(label < 1.5, table[first + 1], table[first + 2]))

    last = info_row(size)
    def prepare(y_block):
        found = {}
        for x_block in set(order):
            block = 4 * x_block + y_block
            if block == 0:
                found[x_block] = own[last : last + 16]
                continue
            info = wide(blocks[block][last : last + 16])
            scale = scale_of(info)
            for i in range(3 * ratio):
                at = (3 * ratio * block + i) * TILE
                scales[at : at + TILE] = lane(scale[:TILE], SCALE_AT + i)
            amps = info * pltpu.roll(scale, 128 - ny, 1)
            found[x_block] = jnp.where(iota(1, 16) < ny, info, amps)
        for i, x_block in enumerate(order):
            at = (y_block * len(order) + i) * nx
            sources[at : at + nx] = found[x_block][:nx]

    def load_pair(block, pair, r):
        out = []
        for y in (2 * pair, 2 * pair + 1):
            first, second, third = field_rows(size, y, r)
            if block == 0:
                tiles = [own[first : first + TILE], own[first + TILE : first + 16], own[second : second + TILE]]
            else:
                both = wide(blocks[block][first : first + 16])
                at = second // 16 * 16
                ends = wide(blocks[block][at : at + 16])[second - at : second - at + TILE]
                tiles = [both[:TILE], both[TILE:], ends]
                rows = [((3 * block + i) * ratio + r) * TILE + y for i in range(3)]
                tiles = [t * scales[row : row + 1] for t, row in zip(tiles, rows)]
            out.append(tiles)
        third = field_rows(size, 2 * pair, r)[2]
        if block == 0:
            return out, own[third : third + TILE]
        at = third // 16 * 16
        return out, wide(blocks[block][at : at + 16])[third - at : third - at + TILE]

    def unpack(y_block, pair, to):
        for r in range(ratio):
            held = {x: load_pair(4 * x + y_block, pair, r) for x in set(order)}
            for i, y in enumerate((2 * pair, 2 * pair + 1)):
                outs = []
                for k in range(0, len(order), 2):
                    one, two = order[k], order[k + 1]
                    tiles = [halves((held[one][0][i][j], held[two][0][i][j]), low) for j in range(3)]
                    (ex, ey), (hx, hy), (ez, hz) = tiles
                    label = halves((held[one][1], held[two][1]), low)[i]
                    at = (y_block * len(order) + k) * nx
                    source = sources[pl.ds(at + r, TILE, stride=ratio)]
                    height, amp = lane(source, y), lane(source, ny + y)
                    outs.append(
                        [
                            ex * DT_STEP, ey * DT_STEP, ez * DT_STEP, hx, hy, hz, pick(label, 0), pick(label, 3),
                            jnp.where(lanes.astype(F32) == height, amp, 0.0),
                        ]
                    )
                for j in range(9):
                    tile = jnp.concatenate([o[j] for o in outs], 0) if len(outs) > 1 else outs[0][j]
                    if j < 3:
                        electric[to + i, j * ratio + r] = tile
                    elif j < 6:
                        magnetic[to + i, (j - 3) * ratio + r] = tile
                    else:
                        (coef, gain_out, profile)[j - 6][to + i, r] = tile

    for y_block, pieces in enumerate(places(parity[0], ny)):
        prepare(y_block)
        for first, count, to in pieces:
            for j in range(0, count, 2):
                unpack(y_block, (first + j) // 2, to + j)

    base_steps(size, range(FIRST_STEPS), coef, profile, moves, (electric, magnetic), (electric, magnetic))


def later_kernel(size, coef, profile, electric, magnetic, moves, electric_held, magnetic_held):
    base_steps(
        size, range(FIRST_STEPS, STEPS), coef, profile, moves, (electric, magnetic), (electric_held, magnetic_held)
    )


def base_steps(size, steps, coef, profile, moves, fields, held):
    nx, ny = size
    ratio = nx // GROUP
    to_electric, to_magnetic = held
    moved = 0
    for step in steps:
        electric, magnetic = fields if step == steps[0] else held
        wave = math.cos(OMEGA_FREQ * (step + 0.5) * DT_STEP)
        first, end = rows_of(step, ny)
        now = load_row(electric, first - 1, ratio)
        above = load_row(electric, first, ratio)
        new = add_curl_forward(load_row(magnetic, first - 1, ratio), now, above)
        below_x, below_z = new[0], new[2]
        for run in chunks(first, end):
            field = [above] + [load_row(electric, at + 1, ratio) for at in run]
            above = field[-1]
            new = [
                add_curl_forward(load_row(magnetic, at, ratio), field[i], field[i + 1])
                for i, at in enumerate(run)
            ]
            for i, at in enumerate(run):
                drive = curl_backward(new[i], below_x, below_z)
                below_x, below_z = new[i][0], new[i][2]
                drive[2] = [d + wave * profile[at, r] for r, d in enumerate(drive[2])]
                change = [[coef[at, r] * drive[c][r] for r in range(ratio)] for c in range(3)]
                store_row(moves, at - first + moved, change)
                if step < STEPS - 1:
                    store_row(to_magnetic, at, new[i])
                    store_row(
                        to_electric, at,
                        [[p + q for p, q in zip(field[i][c], change[c])] for c in range(3)],
                    )
        moved += end - first


def tangent_kernel(size, order, parity, coef, gain, moves_first, moves_later, own, *rest):
    nx, ny = size
    ratio, plane = nx // GROUP, nx * ny
    n_blocks = 4 * len(set(order)) - 1
    blocks, rest = (own,) + rest[:n_blocks], rest[n_blocks:]
    out_e, out_h, electric, magnetic, weight = rest
    low = iota(0) < GROUP

    scales = [None if i == 0 else scale_of(wide(b[plane : plane + 16])) for i, b in enumerate(blocks)]

    def unpack(y_block, pair, to, wanted):
        loaded = {}
        for x_block in order:
            i = 4 * x_block + y_block
            if x_block in loaded:
                continue
            tiles = []
            for r in range(ratio):
                unit = pair * ratio + r
                if i == 0:
                    tiles.append(own[TILE * unit : TILE * unit + TILE])
                else:
                    at = TILE * unit // 16 * 16
                    both = wide(blocks[i][at : at + 16])
                    half = TILE * unit - at
                    tiles.append(both[half : half + TILE] * scales[i][unit : unit + 1])
            loaded[x_block] = tiles
        for r in range(ratio):
            outs = [
                halves((loaded[order[k]][r], loaded[order[k + 1]][r]), low)
                for k in range(0, len(order), 2)
            ]
            for i in wanted:
                tile = jnp.concatenate([o[i] for o in outs], 0) if len(outs) > 1 else outs[0][i]
                weight[to + i, r] = tile * gain[to + i, r]

    for y_block, pieces in enumerate(places(parity[0], ny)):
        for first, count, to in pieces:
            for j in range(0, count, 2):
                unpack(y_block, (first + j) // 2, to + j, (0, 1))

    moved = 0
    for step in range(STEPS):
        first, end = rows_of(step, ny)
        if step == FIRST_STEPS:
            moved = 0
        moves = moves_first if step < FIRST_STEPS else moves_later
        shift = moved - first
        if step == 0:

            for at in range(first, end):
                change = load_row(moves, at + shift, ratio)
                store_row(electric, at, [[-(weight[at, r] * change[c][r]) for r in range(ratio)] for c in range(3)])
        else:

            def old(at, step=step):
                return load_row(magnetic, at, ratio) if step > 1 else None

            now = load_row(electric, first - 1, ratio)
            above = load_row(electric, first, ratio)
            new = add_curl_forward(old(first - 1), now, above)

            below_x, below_z = new[0], new[2]
            for run in chunks(first, end):
                field = [above] + [load_row(electric, at + 1, ratio) for at in run]
                above = field[-1]
                new = [add_curl_forward(old(at), field[i], field[i + 1]) for i, at in enumerate(run)]
                for i, at in enumerate(run):
                    curl = curl_backward(new[i], below_x, below_z)
                    below_x, below_z = new[i][0], new[i][2]
                    change = load_row(moves, at + shift, ratio)
                    store_row(magnetic, at, new[i])
                    store_row(
                        electric, at,
                        [
                            [
                                field[i][c][r] + (coef[at, r] * curl[c][r] - weight[at, r] * change[c][r])
                                for r in range(ratio)
                            ]
                            for c in range(3)
                        ],
                    )
        moved += end - first

    at_own = GROUP * order.index(0)
    stride = ratio * ny
    for y in range(ny):
        for r in range(ratio):
            for out, ref, factor in ((out_e, electric, 1.0 / DT_STEP), (out_h, magnetic, None)):
                for c in range(3):
                    tile = ref[STEPS + y, c * ratio + r, at_own : at_own + GROUP]
                    out[pl.ds(c * plane + r * ny + y, GROUP, stride=stride)] = tile if factor is None else tile * factor


def call(kernel, name, outs, specs, scratch, about_us, args, vmem=VMEM_LIMIT):
    return pl.pallas_call(
        kernel,
        out_shape=outs,
        in_specs=specs,
        out_specs=tuple(pl.BlockSpec(memory_space=pltpu.VMEM) for _ in outs),
        scratch_shapes=scratch,
        compiler_params=pltpu.CompilerParams(vmem_limit_bytes=vmem),
        cost_estimate=pl.CostEstimate(flops=int(about_us * 1e9), bytes_accessed=0, transcendentals=0),
        name=name,
    )(*args)


def body(sizes, e_init, h_init, eps_levels, region_gain, region_labels, kl_blocks, kl_modes, source_z, source_amp):
    n_gx, n_gy, n_mode = sizes
    _, nx, ny, nz = e_init.shape
    assert n_gy == 4 and n_mode == 4 and ny == TILE and nx <= 16 and nx % GROUP == 0 and nx >= STEPS and ny < STEPS < 2 * ny
    ratio, plane = nx // GROUP, nx * ny
    size = (nx, ny)
    vmem, smem, hbm = (pl.BlockSpec(memory_space=s) for s in (pltpu.VMEM, pltpu.SMEM, pltpu.HBM))
    f32 = lambda *shape: jax.ShapeDtypeStruct(shape, F32)
    i16 = lambda *shape: jax.ShapeDtypeStruct(shape, jnp.int16)

    def over_xy(block, dx, flip):
        route = [
            (gx * n_gy + gy, (gx + dx) % n_gx * n_gy + (gy ^ flip))
            for gx in range(n_gx)
            for gy in range(n_gy)
        ]
        return lax.ppermute(block, ("gx", "gy"), route)

    def over_mode(block, flip):
        return lax.ppermute(block, "mode", [(i, i ^ flip) for i in range(n_mode)])

    me = lax.axis_index("mode").astype(jnp.int32).reshape(1)
    parity = (lax.axis_index("gy") % 2).astype(jnp.int32).reshape(1)
    packed, own, own_part, near_part, tables, far_parts = call(
        functools.partial(pack_kernel, size), "pack",
        (
            i16(info_row(size) + 16, nz), f32(info_row(size) + 16, nz), f32(plane, nz), f32(plane, nz), f32(TILE, nz),
            i16(2 * (plane + 16), nz),
        ),
        [smem] + [hbm] * 9,
        [pltpu.SMEM(a.shape, a.dtype) for a in (kl_modes, eps_levels, region_gain)]
        + [pltpu.VMEM((3 * plane, nz), F32)] * 2
        + [pltpu.VMEM((plane, nz), jnp.int32), pltpu.VMEM((kl_blocks.shape[0] * plane, nz), kl_blocks.dtype)]
        + [pltpu.VMEM((ny, nx), jnp.int32), pltpu.VMEM((ny, nx), F32), pltpu.VMEM((2 * plane, nz), F32)]
        + [pltpu.SemaphoreType.DMA((9,))],
        1.5,
        (
            me,
            *(
                pltpu.with_memory_space_constraint(a, pltpu.HBM)
                for a in (
                    kl_modes, eps_levels, region_gain, e_init.reshape(-1, nz), h_init.reshape(-1, nz),
                    region_labels.reshape(-1, nz), kl_blocks.reshape(-1, nz), source_z.T, source_amp.T,
                )
            ),
        ),
    )

    moves_x = [0, -1] if n_gx == 2 else [0, -1, 1]
    order = (0, 1) if n_gx == 2 else (2, 0, 1, 1)
    groups = GROUP * len(order)

    def gather(block):
        near = [block] + [over_xy(block, dx, 0) for dx in moves_x[1:]]
        far = [over_xy(block, dx, 2) for dx in moves_x]
        return near, far

    far_parts = over_mode(far_parts, 1)
    (near_part,) = call(
        functools.partial(half_kernel, size), "half",
        (i16(plane + 16, nz),), [vmem] * 2, [], 0.2, (near_part, far_parts),
    )
    near_part = over_mode(near_part, 2)
    near, far = gather(packed)

    def with_core(near, far):
        got = near + far
        sent = over_xy(jnp.concatenate(got, 0), 0, 1)
        rows = got[0].shape[0]
        other = [sent[rows * i : rows * i + rows] for i in range(len(got))]
        other_near, other_far = other[: len(near)], other[len(near) :]
        return [b for four in zip(near, other_near, far, other_far) for b in four]

    deps_packed, deps_own = call(
        functools.partial(sum_kernel, size), "sum",
        (i16(plane + 16, nz), f32(plane, nz)), [vmem] * 3, [pltpu.VMEM((3 * plane, nz), F32)],
        1.2, (own_part, far_parts, near_part),
    )
    far, near, deps_packed = lax.optimization_barrier((far[::-1], near, deps_packed))
    far = far[::-1]
    blocks = with_core(near, far)
    rows = ny + 2 * STEPS
    counts = [rows_of(step, ny)[1] - rows_of(step, ny)[0] for step in range(STEPS)]
    moved = [sum(counts[:FIRST_STEPS]), sum(counts[FIRST_STEPS:])]
    plane_shape, field_shape = (rows, ratio, groups, nz), (rows, 3 * ratio, groups, nz)
    deps_near, deps_far = gather(deps_packed)
    coef, gain, moves_first, electric, magnetic, profile = call(
        functools.partial(base_kernel, size, order), "base",
        (f32(*plane_shape), f32(*plane_shape), f32(moved[0], *field_shape[1:]), f32(*field_shape), f32(*field_shape), f32(*plane_shape)),
        [smem] + [vmem] * (1 + len(blocks)),
        [pltpu.VMEM((12 * ratio * len(set(order)) * TILE, nz), F32), pltpu.VMEM((4 * len(order) * nx, nz), F32)],
        3.5, (parity, tables, own, *blocks[1:]),
    )
    deps_far, deps_near, coef, gain, moves_first = lax.optimization_barrier(
        (deps_far[::-1], deps_near, coef, gain, moves_first)
    )
    deps = with_core(deps_near, deps_far[::-1])
    (moves_later,) = call(
        functools.partial(later_kernel, size), "later",
        (f32(moved[1], *field_shape[1:]),), [vmem] * 4, [pltpu.VMEM(field_shape, F32)] * 2,
        1.5, (coef, profile, electric, magnetic),
    )
    out_e, out_h = call(
        functools.partial(tangent_kernel, size, order), "tangent",
        (f32(3 * plane, nz), f32(3 * plane, nz)),
        [smem] + [vmem] * (4 + len(deps)),
        [pltpu.VMEM(field_shape, F32)] * 2 + [pltpu.VMEM(plane_shape, F32)],
        4.0, (parity, coef, gain, moves_first, moves_later, deps_own, *deps[1:]),
    )
    shape = (1, 3, nx, ny, nz)
    return out_e.reshape(shape), out_h.reshape(shape)


def solution(mesh):
    placed = (
        P(None, "gx", "gy", None),
        P(None, "gx", "gy", None),
        P(),
        P(),
        P("gx", "gy", None),
        P("mode", "gx", "gy", None),
        P(),
        P("gx", "gy"),
        P("gx", "gy"),
    )
    return jax.shard_map(
        functools.partial(body, tuple(mesh.shape[a] for a in ("gx", "gy", "mode"))),
        mesh=mesh,
        in_specs=placed,
        out_specs=(P("mode", None, "gx", "gy", None), P("mode", None, "gx", "gy", None)),
        check_vma=False,
    )
```

```python
import functools
import math

import jax
import jax.numpy as jnp
from jax import lax
from jax.experimental import pallas as pl
from jax.experimental.pallas import tpu as pltpu
from jax.sharding import PartitionSpec as P

STEPS = 10
DT_STEP = 0.99 / math.sqrt(3.0)
OMEGA_FREQ = 0.7

GROUP = 4
TILE = 8
FULL = 32000.0
FINE = 256.0
FIRST_STEPS = 4
SCALE_AT = 4 * 8
CHUNK = 13
F32 = jnp.float32
VMEM_LIMIT = 24 * 1024 * 1024


def iota(axis, rows=TILE):
    return lax.broadcasted_iota(jnp.int32, (rows, 128), axis)


def scale_code(largest):
    return jnp.clip(jnp.ceil(jnp.log2(largest) * FINE) + 1.0, -FULL, FULL)


def to_codes(values, code):
    return jnp.round(values * (jnp.exp2(code * (-1.0 / FINE)) * FULL))


def scale_of(code):
    return jnp.exp2(code * (1.0 / FINE)) * (1.0 / FULL)


def narrow(tiles):
    return jnp.concatenate(tiles, 0).astype(jnp.int32).astype(jnp.int16)


def wide(codes):
    return codes.astype(jnp.int32).astype(F32)


def lane(tile, at):
    return jnp.broadcast_to(tile[:, at : at + 1], tile.shape)


def code_tiles(total, k, codes):
    rows, coded = iota(0, 16), []
    for i in range(2):
        tile = total[TILE * i : TILE * i + TILE]
        code = scale_code(jnp.max(jnp.abs(tile), axis=(0, 1), keepdims=True))
        coded.append(to_codes(tile, code))
        codes = jnp.where(rows == 2 * k + i, code, codes)
    return narrow(coded), codes


def decoded(part, at, plane, k):
    scales = scale_of(wide(part[at + plane : at + plane + 16]))
    coded = wide(part[at + 16 * k : at + 16 * k + 16])
    return [coded[TILE * i : TILE * i + TILE] * scales[2 * k + i : 2 * k + i + 1] for i in range(2)]


def half_kernel(size, near_part, far_parts, part):
    plane = size[0] * size[1]
    codes = jnp.zeros((16, 128), F32)
    for k in range(plane // 16):
        total = near_part[16 * k : 16 * k + 16] + jnp.concatenate(decoded(far_parts, plane + 16, plane, k), 0)
        part[16 * k : 16 * k + 16], codes = code_tiles(total, k, codes)
    part[plane:] = narrow([codes])


def field_rows(size, y, r):
    nx, ny = size
    ratio = nx // GROUP
    second, third = 16 * ny * ratio, 24 * ny * ratio
    return (
        (y * ratio + r) * 16,
        second + (y // 2 * ratio + r) * 16 + y % 2 * TILE,
        third + (y // 4 * ratio + r) * 16 + y % 4 * GROUP,
    )


def info_row(size):
    nx, ny = size
    return 28 * ny * (nx // GROUP)


def pack_kernel(
    size, me, modes_at, levels_at, gains_at, e_at, h_at, labels_at, kl_at, z_at, amp_at,
    packed, own, own_part, near_part, tables, far_parts, *rest,
):
    nx, ny = size
    modes, levels, gains, e, h, labels, kl, source_z, source_amp, label_rows, sems = rest
    ratio, plane, stride = nx // GROUP, nx * ny, nx // GROUP * ny
    ends = zip(
        (modes_at, levels_at, gains_at, kl_at, e_at, h_at, labels_at, z_at, amp_at),
        (modes, levels, gains, kl, e, h, labels, source_z, source_amp),
    )
    copies = [pltpu.make_async_copy(there, here, sems.at[i]) for i, (there, here) in enumerate(ends)]
    for copy in copies:
        copy.start()
    label_rows[plane:] = jnp.zeros((plane, 128), F32)
    for copy in copies[:4]:
        copy.wait()
    for i in range(3):
        at = slice(i, i + 1)
        tables[at] = jnp.full((1, 128), DT_STEP * DT_STEP) / jnp.full((1, 128), levels[i])
        tables[slice(i + 3, i + 4)] = jnp.full((1, 128), gains[i]) / jnp.full((1, 128), levels[i])
    tables[6:8] = jnp.zeros((2, 128), F32)
    low, lanes = iota(0) < GROUP, iota(1)

    blocks = kl.shape[0] // plane
    weights = [
        [(modes[me[0] * blocks + j] == (me[0] ^ d)).astype(F32) for j in range(blocks)] for d in (0, 2, 1, 3)
    ]
    codes = [jnp.zeros((16, 128), F32) for _ in range(2)]
    for k in range(plane // 16):
        tiles = [kl[j * plane + 16 * k : j * plane + 16 * k + 16].astype(F32) for j in range(blocks)]
        for d in range(4):
            total = sum(weights[d][j] * tiles[j] for j in range(blocks))
            if d < 2:
                (own_part, near_part)[d][16 * k : 16 * k + 16] = total
            else:
                first = (plane + 16) * (d - 2) + 16 * k
                far_parts[first : first + 16], codes[d - 2] = code_tiles(total, k, codes[d - 2])
    for i in range(2):
        first = (plane + 16) * i + plane
        far_parts[first : first + 16] = narrow([codes[i]])

    for copy in copies[4:]:
        copy.wait()
    label_rows[:plane] = labels[...].astype(F32)
    heights_of = source_z[...].astype(F32)
    amps_of = source_amp[...]
    info = jnp.zeros((TILE, 128), F32)
    rows = iota(0)
    for r in range(ratio):
        labels_held = []
        for y in range(ny):
            at = r * ny + y
            tiles = [e[pl.ds(at, TILE, stride=stride)], h[pl.ds(at, TILE, stride=stride)]]
            e_last = e[pl.ds(at + plane, TILE, stride=stride)]
            h_last = h[pl.ds(at + plane, TILE, stride=stride)]
            tiles.append(jnp.where(low, pltpu.roll(e_last, GROUP, 0), h_last))
            coded = []
            for i, tile in enumerate(tiles):
                code = scale_code(jnp.max(jnp.abs(tile), axis=(0, 1), keepdims=True))
                coded.append(to_codes(tile, code))
                info = jnp.where((rows == y) & (lanes == SCALE_AT + i * ratio + r), code, info)
            first, second, third = field_rows(size, y, r)
            packed[first : first + 16] = narrow(coded[:2])
            own[first : first + TILE] = tiles[0]
            own[first + TILE : first + 16] = tiles[1]
            own[second : second + TILE] = tiles[2]
            labels_held.append(label_rows[pl.ds(at, TILE, stride=stride)])
            if y % 2 == 0:
                last_even = coded[2]
                continue
            packed[second - TILE : second + TILE] = narrow([last_even, coded[2]])
            pair = jnp.where(low, labels_held[-2], pltpu.roll(labels_held[-1], GROUP, 0))
            labels_held[-2:] = [pair]
            third = third // TILE * TILE
            own[third : third + TILE] = pair
            if len(labels_held) == 2:
                packed[third - TILE : third + TILE] = narrow(labels_held)
                labels_held = []
    amp_codes = scale_code(jnp.abs(amps_of))
    sources = [heights_of, to_codes(amps_of, amp_codes), amp_codes, amps_of]
    sources = jnp.concatenate([jnp.concatenate(sources, 0), jnp.zeros((4 * ny, 128 - nx), F32)], 1)
    sources = jnp.concatenate([sources, jnp.zeros((128 - 4 * ny, 128), F32)], 0).T[:16]
    lanes16 = iota(1, 16)
    last = info_row(size)
    info = jnp.concatenate([info, jnp.zeros((TILE, 128), F32)], 0)
    packed[last : last + 16] = jnp.where(lanes16 < 3 * ny, sources, info).astype(jnp.int32).astype(jnp.int16)
    own[last : last + 16] = jnp.where(lanes16 < ny, sources, pltpu.roll(sources, 128 - 2 * ny, 1))


def sum_kernel(size, own_part, far_parts, near_part, packed, own, total):
    nx, ny = size
    ratio, plane, stride = nx // GROUP, nx * ny, nx // GROUP * ny
    total[:plane] = jnp.zeros((plane, 128), F32)
    total[2 * plane :] = jnp.zeros((plane, 128), F32)
    for k in range(plane // 16):
        both = zip(decoded(far_parts, 0, plane, k), decoded(near_part, 0, plane, k))
        for i, (far, near) in enumerate(both):
            at = 16 * k + TILE * i
            total[plane + at : plane + at + TILE] = own_part[at : at + TILE] + far + near
    low, rows16 = iota(0) < GROUP, iota(0, 16)
    codes = jnp.zeros((16, 128), F32)
    held = []
    for pair in range(ny // 2):
        for r in range(ratio):
            at = r * ny + 2 * pair
            even = total[pl.ds(plane + at, TILE, stride=stride)]
            odd = total[pl.ds(at + 1, TILE, stride=stride)]
            tile = jnp.where(low, even, odd)
            unit = pair * ratio + r
            own[TILE * unit : TILE * unit + TILE] = tile
            code = scale_code(jnp.max(jnp.abs(tile), axis=(0, 1), keepdims=True))
            codes = jnp.where(rows16 == unit, code, codes)
            held.append(to_codes(tile, code))
            if len(held) == 2:
                packed[TILE * (unit - 1) : TILE * (unit + 1)] = narrow(held)
                held = []
    packed[plane:] = narrow([codes])


def x_up(tiles):
    rows = tiles[0].shape[0]
    return tiles[1:] + [pltpu.roll(tiles[0], rows - 1, 0)]


def x_down(tiles):
    return [pltpu.roll(tiles[-1], 1, 0)] + tiles[:-1]


def z_up(tiles):
    last = iota(1, tiles[0].shape[0]) == 127
    return [jnp.where(last, 0.0, pltpu.roll(t, 127, 1)) for t in tiles]


def z_down(tiles):
    first = iota(1, tiles[0].shape[0]) == 0
    return [jnp.where(first, 0.0, pltpu.roll(t, 1, 1)) for t in tiles]


def add_curl_forward(magnetic, now, above):
    ex, ey, ez = now
    above_x, _, above_z = above
    ups = (z_up(ex), z_up(ey), x_up(ey), x_up(ez))
    out = [[], [], []]
    for r in range(len(ex)):
        curl = (
            (above_z[r] - ez[r]) - (ups[1][r] - ey[r]),
            (ups[0][r] - ex[r]) - (ups[3][r] - ez[r]),
            (ups[2][r] - ey[r]) - (above_x[r] - ex[r]),
        )
        for c in range(3):
            out[c].append(-curl[c] if magnetic is None else magnetic[c][r] - curl[c])
    return out


def curl_backward(now, below_x, below_z):
    hx, hy, hz = now
    downs = (z_down(hx), z_down(hy), x_down(hy), x_down(hz))
    out = [[], [], []]
    for r in range(len(hx)):
        out[0].append((hz[r] - below_z[r]) - (hy[r] - downs[1][r]))
        out[1].append((hx[r] - downs[0][r]) - (hz[r] - downs[3][r]))
        out[2].append((hy[r] - downs[2][r]) - (hx[r] - below_x[r]))
    return out


def load_row(ref, at, ratio):
    return [[ref[at, c * ratio + r] for r in range(ratio)] for c in range(3)]


def store_row(ref, at, row):
    ratio = len(row[0])
    for c in range(3):
        for r in range(ratio):
            ref[at, c * ratio + r] = row[c][r]


def flat(row):
    return [t for tiles in row for t in tiles]


def rows_of(step, ny):
    return step + 1, ny + 2 * STEPS - 1 - step


def chunks(first, end):
    count = -(-(end - first) // CHUNK)
    cuts = [first + (end - first) * i // count for i in range(count + 1)]
    return [range(*cut) for cut in zip(cuts, cuts[1:])]


def places(parity, ny):
    upper, lower = STEPS + ny, STEPS - ny
    one = jnp.where(parity == 0, upper, lower)
    three = jnp.where(parity == 0, lower, upper)
    over = STEPS - ny
    return (
        ((0, ny, STEPS),),
        ((0, ny, one),),
        ((ny - over, over, 0), (0, over, STEPS + 2 * ny)),
        ((0, ny, three),),
    )


def halves(pairs, low):
    one, two = pairs
    return [
        jnp.where(low, one, pltpu.roll(two, GROUP, 0)),
        jnp.where(low, pltpu.roll(one, GROUP, 0), two),
    ]


def base_kernel(size, order, parity, tables, own, *rest):
    nx, ny = size
    ratio = nx // GROUP
    blocks, rest = rest[:-8], rest[-8:]
    coef, gain_out, moves, electric, magnetic, profile, scales, sources = rest
    blocks = (own,) + blocks
    low, lanes = iota(0) < GROUP, iota(1)
    table = [jnp.broadcast_to(tables[i : i + 1], (TILE, 128)) for i in range(6)]

    def pick(label, first):
        return jnp.where(label < 0.5, table[first], jnp.where(label < 1.5, table[first + 1], table[first + 2]))

    last = info_row(size)
    def prepare(y_block):
        found = {}
        for x_block in set(order):
            block = 4 * x_block + y_block
            if block == 0:
                found[x_block] = own[last : last + 16]
                continue
            info = wide(blocks[block][last : last + 16])
            scale = scale_of(info)
            for i in range(3 * ratio):
                at = (3 * ratio * block + i) * TILE
                scales[at : at + TILE] = lane(scale[:TILE], SCALE_AT + i)
            amps = info * pltpu.roll(scale, 128 - ny, 1)
            found[x_block] = jnp.where(iota(1, 16) < ny, info, amps)
        for i, x_block in enumerate(order):
            at = (y_block * len(order) + i) * nx
            sources[at : at + nx] = found[x_block][:nx]

    def load_pair(block, pair, r):
        out = []
        for y in (2 * pair, 2 * pair + 1):
            first, second, third = field_rows(size, y, r)
            if block == 0:
                tiles = [own[first : first + TILE], own[first + TILE : first + 16], own[second : second + TILE]]
            else:
                both = wide(blocks[block][first : first + 16])
                at = second // 16 * 16
                ends = wide(blocks[block][at : at + 16])[second - at : second - at + TILE]
                tiles = [both[:TILE], both[TILE:], ends]
                rows = [((3 * block + i) * ratio + r) * TILE + y for i in range(3)]
                tiles = [t * scales[row : row + 1] for t, row in zip(tiles, rows)]
            out.append(tiles)
        third = field_rows(size, 2 * pair, r)[2]
        if block == 0:
            return out, own[third : third + TILE]
        at = third // 16 * 16
        return out, wide(blocks[block][at : at + 16])[third - at : third - at + TILE]

    def unpack(y_block, pair, to):
        for r in range(ratio):
            held = {x: load_pair(4 * x + y_block, pair, r) for x in set(order)}
            for i, y in enumerate((2 * pair, 2 * pair + 1)):
                outs = []
                for k in range(0, len(order), 2):
                    one, two = order[k], order[k + 1]
                    tiles = [halves((held[one][0][i][j], held[two][0][i][j]), low) for j in range(3)]
                    (ex, ey), (hx, hy), (ez, hz) = tiles
                    label = halves((held[one][1], held[two][1]), low)[i]
                    at = (y_block * len(order) + k) * nx
                    source = sources[pl.ds(at + r, TILE, stride=ratio)]
                    height, amp = lane(source, y), lane(source, ny + y)
                    outs.append(
                        [
                            ex * DT_STEP, ey * DT_STEP, ez * DT_STEP, hx, hy, hz, pick(label, 0), pick(label, 3),
                            jnp.where(lanes.astype(F32) == height, amp, 0.0),
                        ]
                    )
                for j in range(9):
                    tile = jnp.concatenate([o[j] for o in outs], 0) if len(outs) > 1 else outs[0][j]
                    if j < 3:
                        electric[to + i, j * ratio + r] = tile
                    elif j < 6:
                        magnetic[to + i, (j - 3) * ratio + r] = tile
                    else:
                        (coef, gain_out, profile)[j - 6][to + i, r] = tile

    for y_block, pieces in enumerate(places(parity[0], ny)):
        prepare(y_block)
        for first, count, to in pieces:
            for j in range(0, count, 2):
                unpack(y_block, (first + j) // 2, to + j)

    base_steps(size, range(FIRST_STEPS), coef, profile, moves, (electric, magnetic), (electric, magnetic))


def later_kernel(size, coef, profile, electric, magnetic, moves, electric_held, magnetic_held):
    base_steps(
        size, range(FIRST_STEPS, STEPS), coef, profile, moves, (electric, magnetic), (electric_held, magnetic_held)
    )


def base_steps(size, steps, coef, profile, moves, fields, held):
    nx, ny = size
    ratio = nx // GROUP
    to_electric, to_magnetic = held
    moved = 0
    for step in steps:
        electric, magnetic = fields if step == steps[0] else held
        wave = math.cos(OMEGA_FREQ * (step + 0.5) * DT_STEP)
        first, end = rows_of(step, ny)
        now = load_row(electric, first - 1, ratio)
        above = load_row(electric, first, ratio)
        new = add_curl_forward(load_row(magnetic, first - 1, ratio), now, above)
        below_x, below_z = new[0], new[2]
        for run in chunks(first, end):
            field = [above] + [load_row(electric, at + 1, ratio) for at in run]
            above = field[-1]
            new = [
                add_curl_forward(load_row(magnetic, at, ratio), field[i], field[i + 1])
                for i, at in enumerate(run)
            ]
            for i, at in enumerate(run):
                drive = curl_backward(new[i], below_x, below_z)
                below_x, below_z = new[i][0], new[i][2]
                drive[2] = [d + wave * profile[at, r] for r, d in enumerate(drive[2])]
                change = [[coef[at, r] * drive[c][r] for r in range(ratio)] for c in range(3)]
                store_row(moves, at - first + moved, change)
                if step < STEPS - 1:
                    store_row(to_magnetic, at, new[i])
                    store_row(
                        to_electric, at,
                        [[p + q for p, q in zip(field[i][c], change[c])] for c in range(3)],
                    )
        moved += end - first


def tangent_kernel(size, order, parity, coef, gain, moves_first, moves_later, own, *rest):
    nx, ny = size
    ratio, plane = nx // GROUP, nx * ny
    n_blocks = 4 * len(set(order)) - 1
    blocks, rest = (own,) + rest[:n_blocks], rest[n_blocks:]
    out_e, out_h, electric, magnetic, weight = rest
    low = iota(0) < GROUP

    scales = [None if i == 0 else scale_of(wide(b[plane : plane + 16])) for i, b in enumerate(blocks)]

    def unpack(y_block, pair, to, wanted):
        loaded = {}
        for x_block in order:
            i = 4 * x_block + y_block
            if x_block in loaded:
                continue
            tiles = []
            for r in range(ratio):
                unit = pair * ratio + r
                if i == 0:
                    tiles.append(own[TILE * unit : TILE * unit + TILE])
                else:
                    at = TILE * unit // 16 * 16
                    both = wide(blocks[i][at : at + 16])
                    half = TILE * unit - at
                    tiles.append(both[half : half + TILE] * scales[i][unit : unit + 1])
            loaded[x_block] = tiles
        for r in range(ratio):
            outs = [
                halves((loaded[order[k]][r], loaded[order[k + 1]][r]), low)
                for k in range(0, len(order), 2)
            ]
            for i in wanted:
                tile = jnp.concatenate([o[i] for o in outs], 0) if len(outs) > 1 else outs[0][i]
                weight[to + i, r] = tile * gain[to + i, r]

    for y_block, pieces in enumerate(places(parity[0], ny)):
        for first, count, to in pieces:
            for j in range(0, count, 2):
                unpack(y_block, (first + j) // 2, to + j, (0, 1))

    moved = 0
    for step in range(STEPS):
        first, end = rows_of(step, ny)
        if step == FIRST_STEPS:
            moved = 0
        moves = moves_first if step < FIRST_STEPS else moves_later
        shift = moved - first
        if step == 0:

            for at in range(first, end):
                change = load_row(moves, at + shift, ratio)
                store_row(electric, at, [[-(weight[at, r] * change[c][r]) for r in range(ratio)] for c in range(3)])
        else:

            def old(at, step=step):
                return load_row(magnetic, at, ratio) if step > 1 else None

            now = load_row(electric, first - 1, ratio)
            above = load_row(electric, first, ratio)
            new = add_curl_forward(old(first - 1), now, above)

            below_x, below_z = new[0], new[2]
            for run in chunks(first, end):
                field = [above] + [load_row(electric, at + 1, ratio) for at in run]
                above = field[-1]
                new = [add_curl_forward(old(at), field[i], field[i + 1]) for i, at in enumerate(run)]
                for i, at in enumerate(run):
                    curl = curl_backward(new[i], below_x, below_z)
                    below_x, below_z = new[i][0], new[i][2]
                    change = load_row(moves, at + shift, ratio)
                    store_row(magnetic, at, new[i])
                    store_row(
                        electric, at,
                        [
                            [
                                field[i][c][r] + (coef[at, r] * curl[c][r] - weight[at, r] * change[c][r])
                                for r in range(ratio)
                            ]
                            for c in range(3)
                        ],
                    )
        moved += end - first

    at_own = GROUP * order.index(0)
    stride = ratio * ny
    for y in range(ny):
        for r in range(ratio):
            for out, ref, factor in ((out_e, electric, 1.0 / DT_STEP), (out_h, magnetic, None)):
                for c in range(3):
                    tile = ref[STEPS + y, c * ratio + r, at_own : at_own + GROUP]
                    out[pl.ds(c * plane + r * ny + y, GROUP, stride=stride)] = tile if factor is None else tile * factor


def call(kernel, name, outs, specs, scratch, about_us, args, vmem=VMEM_LIMIT):
    return pl.pallas_call(
        kernel,
        out_shape=outs,
        in_specs=specs,
        out_specs=tuple(pl.BlockSpec(memory_space=pltpu.VMEM) for _ in outs),
        scratch_shapes=scratch,
        compiler_params=pltpu.CompilerParams(vmem_limit_bytes=vmem),
        cost_estimate=pl.CostEstimate(flops=int(about_us * 1e9), bytes_accessed=0, transcendentals=0),
        name=name,
    )(*args)


def body(sizes, e_init, h_init, eps_levels, region_gain, region_labels, kl_blocks, kl_modes, source_z, source_amp):
    n_gx, n_gy, n_mode = sizes
    _, nx, ny, nz = e_init.shape
    assert n_gy == 4 and n_mode == 4 and ny == TILE and nx <= 16 and nx % GROUP == 0 and nx >= STEPS and ny < STEPS < 2 * ny
    ratio, plane = nx // GROUP, nx * ny
    size = (nx, ny)
    vmem, smem, hbm = (pl.BlockSpec(memory_space=s) for s in (pltpu.VMEM, pltpu.SMEM, pltpu.HBM))
    f32 = lambda *shape: jax.ShapeDtypeStruct(shape, F32)
    i16 = lambda *shape: jax.ShapeDtypeStruct(shape, jnp.int16)

    def over_xy(block, dx, flip):
        route = [
            (gx * n_gy + gy, (gx + dx) % n_gx * n_gy + (gy ^ flip))
            for gx in range(n_gx)
            for gy in range(n_gy)
        ]
        return lax.ppermute(block, ("gx", "gy"), route)

    def over_mode(block, flip):
        return lax.ppermute(block, "mode", [(i, i ^ flip) for i in range(n_mode)])

    me = lax.axis_index("mode").astype(jnp.int32).reshape(1)
    parity = (lax.axis_index("gy") % 2).astype(jnp.int32).reshape(1)
    packed, own, own_part, near_part, tables, far_parts = call(
        functools.partial(pack_kernel, size), "pack",
        (
            i16(info_row(size) + 16, nz), f32(info_row(size) + 16, nz), f32(plane, nz), f32(plane, nz), f32(TILE, nz),
            i16(2 * (plane + 16), nz),
        ),
        [smem] + [hbm] * 9,
        [pltpu.SMEM(a.shape, a.dtype) for a in (kl_modes, eps_levels, region_gain)]
        + [pltpu.VMEM((3 * plane, nz), F32)] * 2
        + [pltpu.VMEM((plane, nz), jnp.int32), pltpu.VMEM((kl_blocks.shape[0] * plane, nz), kl_blocks.dtype)]
        + [pltpu.VMEM((ny, nx), jnp.int32), pltpu.VMEM((ny, nx), F32), pltpu.VMEM((2 * plane, nz), F32)]
        + [pltpu.SemaphoreType.DMA((9,))],
        1.5,
        (
            me,
            *(
                pltpu.with_memory_space_constraint(a, pltpu.HBM)
                for a in (
                    kl_modes, eps_levels, region_gain, e_init.reshape(-1, nz), h_init.reshape(-1, nz),
                    region_labels.reshape(-1, nz), kl_blocks.reshape(-1, nz), source_z.T, source_amp.T,
                )
            ),
        ),
    )

    moves_x = [0, -1] if n_gx == 2 else [0, -1, 1]
    order = (0, 1) if n_gx == 2 else (2, 0, 1, 1)
    groups = GROUP * len(order)

    def gather(block):
        near = [block] + [over_xy(block, dx, 0) for dx in moves_x[1:]]
        far = [over_xy(block, dx, 2) for dx in moves_x]
        return near, far

    far_parts = over_mode(far_parts, 1)
    (near_part,) = call(
        functools.partial(half_kernel, size), "half",
        (i16(plane + 16, nz),), [vmem] * 2, [], 0.2, (near_part, far_parts),
    )
    near, far = gather(packed)
    near_part = over_mode(near_part, 2)
    *corners, near_part = lax.optimization_barrier((*far[1:], near_part))

    def with_core(near, far):
        got = near + far
        sent = over_xy(jnp.concatenate(got, 0), 0, 1)
        rows = got[0].shape[0]
        other = [sent[rows * i : rows * i + rows] for i in range(len(got))]
        other_near, other_far = other[: len(near)], other[len(near) :]
        return [b for four in zip(near, other_near, far, other_far) for b in four]

    deps_packed, deps_own = call(
        functools.partial(sum_kernel, size), "sum",
        (i16(plane + 16, nz), f32(plane, nz)), [vmem] * 3, [pltpu.VMEM((3 * plane, nz), F32)],
        1.2, (own_part, far_parts, near_part),
    )
    *sides, middle, deps_packed = lax.optimization_barrier((*near[1:], far[0], deps_packed))
    near, far = [packed, *sides], [middle, *corners]
    blocks = with_core(near, far)
    rows = ny + 2 * STEPS
    counts = [rows_of(step, ny)[1] - rows_of(step, ny)[0] for step in range(STEPS)]
    moved = [sum(counts[:FIRST_STEPS]), sum(counts[FIRST_STEPS:])]
    plane_shape, field_shape = (rows, ratio, groups, nz), (rows, 3 * ratio, groups, nz)
    deps_near, deps_far = gather(deps_packed)
    coef, gain, moves_first, electric, magnetic, profile = call(
        functools.partial(base_kernel, size, order), "base",
        (f32(*plane_shape), f32(*plane_shape), f32(moved[0], *field_shape[1:]), f32(*field_shape), f32(*field_shape), f32(*plane_shape)),
        [smem] + [vmem] * (1 + len(blocks)),
        [pltpu.VMEM((12 * ratio * len(set(order)) * TILE, nz), F32), pltpu.VMEM((4 * len(order) * nx, nz), F32)],
        3.5, (parity, tables, own, *blocks[1:]),
    )
    deps_far, deps_near, coef, gain, moves_first = lax.optimization_barrier(
        (deps_far[::-1], deps_near, coef, gain, moves_first)
    )
    deps = with_core(deps_near, deps_far[::-1])
    (moves_later,) = call(
        functools.partial(later_kernel, size), "later",
        (f32(moved[1], *field_shape[1:]),), [vmem] * 4, [pltpu.VMEM(field_shape, F32)] * 2,
        1.5, (coef, profile, electric, magnetic),
    )
    out_e, out_h = call(
        functools.partial(tangent_kernel, size, order), "tangent",
        (f32(3 * plane, nz), f32(3 * plane, nz)),
        [smem] + [vmem] * (4 + len(deps)),
        [pltpu.VMEM(field_shape, F32)] * 2 + [pltpu.VMEM(plane_shape, F32)],
        4.0, (parity, coef, gain, moves_first, moves_later, deps_own, *deps[1:]),
    )
    shape = (1, 3, nx, ny, nz)
    return out_e.reshape(shape), out_h.reshape(shape)


def solution(mesh):
    placed = (
        P(None, "gx", "gy", None),
        P(None, "gx", "gy", None),
        P(),
        P(),
        P("gx", "gy", None),
        P("mode", "gx", "gy", None),
        P(),
        P("gx", "gy"),
        P("gx", "gy"),
    )
    return jax.shard_map(
        functools.partial(body, tuple(mesh.shape[a] for a in ("gx", "gy", "mode"))),
        mesh=mesh,
        in_specs=placed,
        out_specs=(P("mode", None, "gx", "gy", None), P("mode", None, "gx", "gy", None)),
        check_vma=False,
    )
```

```python
import functools
import math

import jax
import jax.numpy as jnp
from jax import lax
from jax.experimental import pallas as pl
from jax.experimental.pallas import tpu as pltpu
from jax.sharding import PartitionSpec as P

STEPS = 10
DT_STEP = 0.99 / math.sqrt(3.0)
OMEGA_FREQ = 0.7

GROUP = 4
TILE = 8
FULL = 32000.0
FINE = 256.0
FIRST_STEPS = 4
SCALE_AT = 4 * 8
CHUNK = 13
F32 = jnp.float32
VMEM_LIMIT = 24 * 1024 * 1024


def iota(axis, rows=TILE):
    return lax.broadcasted_iota(jnp.int32, (rows, 128), axis)


def scale_code(largest):
    return jnp.clip(jnp.ceil(jnp.log2(largest) * FINE) + 1.0, -FULL, FULL)


def to_codes(values, code):
    return jnp.round(values * (jnp.exp2(code * (-1.0 / FINE)) * FULL))


def scale_of(code):
    return jnp.exp2(code * (1.0 / FINE)) * (1.0 / FULL)


def narrow(tiles):
    return jnp.concatenate(tiles, 0).astype(jnp.int32).astype(jnp.int16)


def wide(codes):
    return codes.astype(jnp.int32).astype(F32)


def lane(tile, at):
    return jnp.broadcast_to(tile[:, at : at + 1], tile.shape)


def code_tiles(total, k, codes):
    rows, coded = iota(0, 16), []
    for i in range(2):
        tile = total[TILE * i : TILE * i + TILE]
        code = scale_code(jnp.max(jnp.abs(tile), axis=(0, 1), keepdims=True))
        coded.append(to_codes(tile, code))
        codes = jnp.where(rows == 2 * k + i, code, codes)
    return narrow(coded), codes


def decoded(part, at, scales, k):
    coded = wide(part[at + 16 * k : at + 16 * k + 16])
    return [coded[TILE * i : TILE * i + TILE] * scales[2 * k + i : 2 * k + i + 1] for i in range(2)]


def half_kernel(size, near_part, far_parts, part, scales):
    plane = size[0] * size[1]
    codes = jnp.zeros((16, 128), F32)
    scales[...] = scale_of(wide(far_parts[2 * plane + 16 :]))
    for k in range(plane // 16):
        total = near_part[16 * k : 16 * k + 16] + jnp.concatenate(decoded(far_parts, plane + 16, scales, k), 0)
        part[16 * k : 16 * k + 16], codes = code_tiles(total, k, codes)
    part[plane:] = narrow([codes])


def field_rows(size, y, r):
    nx, ny = size
    ratio = nx // GROUP
    second, third = 16 * ny * ratio, 24 * ny * ratio
    return (
        (y * ratio + r) * 16,
        second + (y // 2 * ratio + r) * 16 + y % 2 * TILE,
        third + (y // 4 * ratio + r) * 16 + y % 4 * GROUP,
    )


def info_row(size):
    nx, ny = size
    return 28 * ny * (nx // GROUP)


def pack_kernel(
    size, me, modes_at, levels_at, gains_at, e_at, h_at, labels_at, kl_at, z_at, amp_at,
    packed, own, own_part, near_part, tables, far_parts, *rest,
):
    nx, ny = size
    modes, levels, gains, e, h, labels, kl, source_z, source_amp, label_rows, sems = rest
    ratio, plane, stride = nx // GROUP, nx * ny, nx // GROUP * ny
    ends = zip(
        (modes_at, levels_at, gains_at, kl_at, e_at, h_at, labels_at, z_at, amp_at),
        (modes, levels, gains, kl, e, h, labels, source_z, source_amp),
    )
    copies = [pltpu.make_async_copy(there, here, sems.at[i]) for i, (there, here) in enumerate(ends)]
    for copy in copies:
        copy.start()
    label_rows[plane:] = jnp.zeros((plane, 128), F32)
    for copy in copies[:4]:
        copy.wait()
    for i in range(3):
        at = slice(i, i + 1)
        tables[at] = jnp.full((1, 128), DT_STEP * DT_STEP) / jnp.full((1, 128), levels[i])
        tables[slice(i + 3, i + 4)] = jnp.full((1, 128), gains[i]) / jnp.full((1, 128), levels[i])
    tables[6:8] = jnp.zeros((2, 128), F32)
    low, lanes = iota(0) < GROUP, iota(1)

    blocks = kl.shape[0] // plane
    weights = [
        [(modes[me[0] * blocks + j] == (me[0] ^ d)).astype(F32) for j in range(blocks)] for d in (0, 2, 1, 3)
    ]
    codes = [jnp.zeros((16, 128), F32) for _ in range(2)]
    for k in range(plane // 16):
        tiles = [kl[j * plane + 16 * k : j * plane + 16 * k + 16].astype(F32) for j in range(blocks)]
        for d in range(4):
            total = sum(weights[d][j] * tiles[j] for j in range(blocks))
            if d < 2:
                (own_part, near_part)[d][16 * k : 16 * k + 16] = total
            else:
                first = (plane + 16) * (d - 2) + 16 * k
                far_parts[first : first + 16], codes[d - 2] = code_tiles(total, k, codes[d - 2])
    for i in range(2):
        first = (plane + 16) * i + plane
        far_parts[first : first + 16] = narrow([codes[i]])

    for copy in copies[4:]:
        copy.wait()
    label_rows[:plane] = labels[...].astype(F32)
    heights_of = source_z[...].astype(F32)
    amps_of = source_amp[...]
    info = jnp.zeros((TILE, 128), F32)
    rows = iota(0)
    for r in range(ratio):
        labels_held = []
        for y in range(ny):
            at = r * ny + y
            tiles = [e[pl.ds(at, TILE, stride=stride)], h[pl.ds(at, TILE, stride=stride)]]
            e_last = e[pl.ds(at + plane, TILE, stride=stride)]
            h_last = h[pl.ds(at + plane, TILE, stride=stride)]
            tiles.append(jnp.where(low, pltpu.roll(e_last, GROUP, 0), h_last))
            coded = []
            for i, tile in enumerate(tiles):
                code = scale_code(jnp.max(jnp.abs(tile), axis=(0, 1), keepdims=True))
                coded.append(to_codes(tile, code))
                info = jnp.where((rows == y) & (lanes == SCALE_AT + i * ratio + r), code, info)
            first, second, third = field_rows(size, y, r)
            packed[first : first + 16] = narrow(coded[:2])
            own[first : first + TILE] = tiles[0]
            own[first + TILE : first + 16] = tiles[1]
            own[second : second + TILE] = tiles[2]
            labels_held.append(label_rows[pl.ds(at, TILE, stride=stride)])
            if y % 2 == 0:
                last_even = coded[2]
                continue
            packed[second - TILE : second + TILE] = narrow([last_even, coded[2]])
            pair = jnp.where(low, labels_held[-2], pltpu.roll(labels_held[-1], GROUP, 0))
            labels_held[-2:] = [pair]
            third = third // TILE * TILE
            own[third : third + TILE] = pair
            if len(labels_held) == 2:
                packed[third - TILE : third + TILE] = narrow(labels_held)
                labels_held = []
    amp_codes = scale_code(jnp.abs(amps_of))
    sources = [heights_of, to_codes(amps_of, amp_codes), amp_codes, amps_of]
    sources = jnp.concatenate([jnp.concatenate(sources, 0), jnp.zeros((4 * ny, 128 - nx), F32)], 1)
    sources = jnp.concatenate([sources, jnp.zeros((128 - 4 * ny, 128), F32)], 0).T[:16]
    lanes16 = iota(1, 16)
    last = info_row(size)
    info = jnp.concatenate([info, jnp.zeros((TILE, 128), F32)], 0)
    packed[last : last + 16] = jnp.where(lanes16 < 3 * ny, sources, info).astype(jnp.int32).astype(jnp.int16)
    own[last : last + 16] = jnp.where(lanes16 < ny, sources, pltpu.roll(sources, 128 - 2 * ny, 1))


def sum_kernel(size, own_part, far_parts, near_part, packed, own, total, far_scales, near_scales):
    nx, ny = size
    ratio, plane, stride = nx // GROUP, nx * ny, nx // GROUP * ny
    far_scales[...] = scale_of(wide(far_parts[plane : plane + 16]))
    near_scales[...] = scale_of(wide(near_part[plane:]))
    total[:plane] = jnp.zeros((plane, 128), F32)
    total[2 * plane :] = jnp.zeros((plane, 128), F32)
    for k in range(plane // 16):
        both = zip(decoded(far_parts, 0, far_scales, k), decoded(near_part, 0, near_scales, k))
        for i, (far, near) in enumerate(both):
            at = 16 * k + TILE * i
            total[plane + at : plane + at + TILE] = own_part[at : at + TILE] + far + near
    low, rows16 = iota(0) < GROUP, iota(0, 16)
    codes = jnp.zeros((16, 128), F32)
    held = []
    for pair in range(ny // 2):
        for r in range(ratio):
            at = r * ny + 2 * pair
            even = total[pl.ds(plane + at, TILE, stride=stride)]
            odd = total[pl.ds(at + 1, TILE, stride=stride)]
            tile = jnp.where(low, even, odd)
            unit = pair * ratio + r
            own[TILE * unit : TILE * unit + TILE] = tile
            code = scale_code(jnp.max(jnp.abs(tile), axis=(0, 1), keepdims=True))
            codes = jnp.where(rows16 == unit, code, codes)
            held.append(to_codes(tile, code))
            if len(held) == 2:
                packed[TILE * (unit - 1) : TILE * (unit + 1)] = narrow(held)
                held = []
    packed[plane:] = narrow([codes])


def x_up(tiles):
    rows = tiles[0].shape[0]
    return tiles[1:] + [pltpu.roll(tiles[0], rows - 1, 0)]


def x_down(tiles):
    return [pltpu.roll(tiles[-1], 1, 0)] + tiles[:-1]


def z_up(tiles):
    last = iota(1, tiles[0].shape[0]) == 127
    return [jnp.where(last, 0.0, pltpu.roll(t, 127, 1)) for t in tiles]


def z_down(tiles):
    first = iota(1, tiles[0].shape[0]) == 0
    return [jnp.where(first, 0.0, pltpu.roll(t, 1, 1)) for t in tiles]


def add_curl_forward(magnetic, now, above):
    ex, ey, ez = now
    above_x, _, above_z = above
    ups = (z_up(ex), z_up(ey), x_up(ey), x_up(ez))
    out = [[], [], []]
    for r in range(len(ex)):
        curl = (
            (above_z[r] - ez[r]) - (ups[1][r] - ey[r]),
            (ups[0][r] - ex[r]) - (ups[3][r] - ez[r]),
            (ups[2][r] - ey[r]) - (above_x[r] - ex[r]),
        )
        for c in range(3):
            out[c].append(-curl[c] if magnetic is None else magnetic[c][r] - curl[c])
    return out


def curl_backward(now, below_x, below_z):
    hx, hy, hz = now
    downs = (z_down(hx), z_down(hy), x_down(hy), x_down(hz))
    out = [[], [], []]
    for r in range(len(hx)):
        out[0].append((hz[r] - below_z[r]) - (hy[r] - downs[1][r]))
        out[1].append((hx[r] - downs[0][r]) - (hz[r] - downs[3][r]))
        out[2].append((hy[r] - downs[2][r]) - (hx[r] - below_x[r]))
    return out


def load_row(ref, at, ratio):
    return [[ref[at, c * ratio + r] for r in range(ratio)] for c in range(3)]


def store_row(ref, at, row):
    ratio = len(row[0])
    for c in range(3):
        for r in range(ratio):
            ref[at, c * ratio + r] = row[c][r]


def flat(row):
    return [t for tiles in row for t in tiles]


def rows_of(step, ny):
    return step + 1, ny + 2 * STEPS - 1 - step


def chunks(first, end):
    count = -(-(end - first) // CHUNK)
    cuts = [first + (end - first) * i // count for i in range(count + 1)]
    return [range(*cut) for cut in zip(cuts, cuts[1:])]


def places(parity, ny):
    upper, lower = STEPS + ny, STEPS - ny
    one = jnp.where(parity == 0, upper, lower)
    three = jnp.where(parity == 0, lower, upper)
    over = STEPS - ny
    return (
        ((0, ny, STEPS),),
        ((0, ny, one),),
        ((ny - over, over, 0), (0, over, STEPS + 2 * ny)),
        ((0, ny, three),),
    )


def halves(pairs, low):
    one, two = pairs
    return [
        jnp.where(low, one, pltpu.roll(two, GROUP, 0)),
        jnp.where(low, pltpu.roll(one, GROUP, 0), two),
    ]


def base_kernel(size, order, parity, tables, own, *rest):
    nx, ny = size
    ratio = nx // GROUP
    blocks, rest = rest[:-8], rest[-8:]
    coef, gain_out, moves, electric, magnetic, profile, scales, sources = rest
    blocks = (own,) + blocks
    low, lanes = iota(0) < GROUP, iota(1)
    table = [jnp.broadcast_to(tables[i : i + 1], (TILE, 128)) for i in range(6)]

    def pick(label, first):
        return jnp.where(label < 0.5, table[first], jnp.where(label < 1.5, table[first + 1], table[first + 2]))

    last = info_row(size)
    def prepare(y_block):
        found = {}
        for x_block in set(order):
            block = 4 * x_block + y_block
            if block == 0:
                found[x_block] = own[last : last + 16]
                continue
            info = wide(blocks[block][last : last + 16])
            scale = scale_of(info)
            for i in range(3 * ratio):
                at = (3 * ratio * block + i) * TILE
                scales[at : at + TILE] = lane(scale[:TILE], SCALE_AT + i)
            amps = info * pltpu.roll(scale, 128 - ny, 1)
            found[x_block] = jnp.where(iota(1, 16) < ny, info, amps)
        for i, x_block in enumerate(order):
            at = (y_block * len(order) + i) * nx
            sources[at : at + nx] = found[x_block][:nx]

    def load_pair(block, pair, r):
        out = []
        for y in (2 * pair, 2 * pair + 1):
            first, second, third = field_rows(size, y, r)
            if block == 0:
                tiles = [own[first : first + TILE], own[first + TILE : first + 16], own[second : second + TILE]]
            else:
                both = wide(blocks[block][first : first + 16])
                at = second // 16 * 16
                ends = wide(blocks[block][at : at + 16])[second - at : second - at + TILE]
                tiles = [both[:TILE], both[TILE:], ends]
                rows = [((3 * block + i) * ratio + r) * TILE + y for i in range(3)]
                tiles = [t * scales[row : row + 1] for t, row in zip(tiles, rows)]
            out.append(tiles)
        third = field_rows(size, 2 * pair, r)[2]
        if block == 0:
            return out, own[third : third + TILE]
        at = third // 16 * 16
        return out, wide(blocks[block][at : at + 16])[third - at : third - at + TILE]

    def unpack(y_block, pair, to):
        for r in range(ratio):
            held = {x: load_pair(4 * x + y_block, pair, r) for x in set(order)}
            for i, y in enumerate((2 * pair, 2 * pair + 1)):
                outs = []
                for k in range(0, len(order), 2):
                    one, two = order[k], order[k + 1]
                    tiles = [halves((held[one][0][i][j], held[two][0][i][j]), low) for j in range(3)]
                    (ex, ey), (hx, hy), (ez, hz) = tiles
                    label = halves((held[one][1], held[two][1]), low)[i]
                    at = (y_block * len(order) + k) * nx
                    source = sources[pl.ds(at + r, TILE, stride=ratio)]
                    height, amp = lane(source, y), lane(source, ny + y)
                    outs.append(
                        [
                            ex * DT_STEP, ey * DT_STEP, ez * DT_STEP, hx, hy, hz, pick(label, 0), pick(label, 3),
                            jnp.where(lanes.astype(F32) == height, amp, 0.0),
                        ]
                    )
                for j in range(9):
                    tile = jnp.concatenate([o[j] for o in outs], 0) if len(outs) > 1 else outs[0][j]
                    if j < 3:
                        electric[to + i, j * ratio + r] = tile
                    elif j < 6:
                        magnetic[to + i, (j - 3) * ratio + r] = tile
                    else:
                        (coef, gain_out, profile)[j - 6][to + i, r] = tile

    for y_block, pieces in enumerate(places(parity[0], ny)):
        prepare(y_block)
        for first, count, to in pieces:
            for j in range(0, count, 2):
                unpack(y_block, (first + j) // 2, to + j)

    base_steps(size, range(FIRST_STEPS), coef, profile, moves, (electric, magnetic), (electric, magnetic))


def later_kernel(size, coef, profile, electric, magnetic, moves, electric_held, magnetic_held):
    base_steps(
        size, range(FIRST_STEPS, STEPS), coef, profile, moves, (electric, magnetic), (electric_held, magnetic_held)
    )


def base_steps(size, steps, coef, profile, moves, fields, held):
    nx, ny = size
    ratio = nx // GROUP
    to_electric, to_magnetic = held
    moved = 0
    for step in steps:
        electric, magnetic = fields if step == steps[0] else held
        wave = math.cos(OMEGA_FREQ * (step + 0.5) * DT_STEP)
        first, end = rows_of(step, ny)
        now = load_row(electric, first - 1, ratio)
        above = load_row(electric, first, ratio)
        new = add_curl_forward(load_row(magnetic, first - 1, ratio), now, above)
        below_x, below_z = new[0], new[2]
        for run in chunks(first, end):
            field = [above] + [load_row(electric, at + 1, ratio) for at in run]
            above = field[-1]
            new = [
                add_curl_forward(load_row(magnetic, at, ratio), field[i], field[i + 1])
                for i, at in enumerate(run)
            ]
            for i, at in enumerate(run):
                drive = curl_backward(new[i], below_x, below_z)
                below_x, below_z = new[i][0], new[i][2]
                drive[2] = [d + wave * profile[at, r] for r, d in enumerate(drive[2])]
                change = [[coef[at, r] * drive[c][r] for r in range(ratio)] for c in range(3)]
                store_row(moves, at - first + moved, change)
                if step < STEPS - 1:
                    store_row(to_magnetic, at, new[i])
                    store_row(
                        to_electric, at,
                        [[p + q for p, q in zip(field[i][c], change[c])] for c in range(3)],
                    )
        moved += end - first


def tangent_kernel(size, order, parity, coef, gain, moves_first, moves_later, own, *rest):
    nx, ny = size
    ratio, plane = nx // GROUP, nx * ny
    n_blocks = 4 * len(set(order)) - 1
    blocks, rest = (own,) + rest[:n_blocks], rest[n_blocks:]
    out_e, out_h, electric, magnetic, weight, scales = rest
    low = iota(0) < GROUP

    for i, block in enumerate(blocks[1:]):
        scales[16 * i : 16 * i + 16] = scale_of(wide(block[plane : plane + 16]))

    def unpack(y_block, pair, to, wanted):
        loaded = {}
        for x_block in order:
            i = 4 * x_block + y_block
            if x_block in loaded:
                continue
            tiles = []
            for r in range(ratio):
                unit = pair * ratio + r
                if i == 0:
                    tiles.append(own[TILE * unit : TILE * unit + TILE])
                else:
                    at = TILE * unit // 16 * 16
                    both = wide(blocks[i][at : at + 16])
                    half = TILE * unit - at
                    row = 16 * (i - 1) + unit
                    tiles.append(both[half : half + TILE] * scales[row : row + 1])
            loaded[x_block] = tiles
        for r in range(ratio):
            outs = [
                halves((loaded[order[k]][r], loaded[order[k + 1]][r]), low)
                for k in range(0, len(order), 2)
            ]
            for i in wanted:
                tile = jnp.concatenate([o[i] for o in outs], 0) if len(outs) > 1 else outs[0][i]
                weight[to + i, r] = tile * gain[to + i, r]

    for y_block, pieces in enumerate(places(parity[0], ny)):
        for first, count, to in pieces:
            for j in range(0, count, 2):
                unpack(y_block, (first + j) // 2, to + j, (0, 1))

    moved = 0
    for step in range(STEPS):
        first, end = rows_of(step, ny)
        if step == FIRST_STEPS:
            moved = 0
        moves = moves_first if step < FIRST_STEPS else moves_later
        shift = moved - first
        if step == 0:

            for at in range(first, end):
                change = load_row(moves, at + shift, ratio)
                store_row(electric, at, [[-(weight[at, r] * change[c][r]) for r in range(ratio)] for c in range(3)])
        else:

            def old(at, step=step):
                return load_row(magnetic, at, ratio) if step > 1 else None

            now = load_row(electric, first - 1, ratio)
            above = load_row(electric, first, ratio)
            new = add_curl_forward(old(first - 1), now, above)

            below_x, below_z = new[0], new[2]
            for run in chunks(first, end):
                field = [above] + [load_row(electric, at + 1, ratio) for at in run]
                above = field[-1]
                new = [add_curl_forward(old(at), field[i], field[i + 1]) for i, at in enumerate(run)]
                for i, at in enumerate(run):
                    curl = curl_backward(new[i], below_x, below_z)
                    below_x, below_z = new[i][0], new[i][2]
                    change = load_row(moves, at + shift, ratio)
                    store_row(magnetic, at, new[i])
                    store_row(
                        electric, at,
                        [
                            [
                                field[i][c][r] + (coef[at, r] * curl[c][r] - weight[at, r] * change[c][r])
                                for r in range(ratio)
                            ]
                            for c in range(3)
                        ],
                    )
        moved += end - first

    at_own = GROUP * order.index(0)
    stride = ratio * ny
    for y in range(ny):
        for r in range(ratio):
            for out, ref, factor in ((out_e, electric, 1.0 / DT_STEP), (out_h, magnetic, None)):
                for c in range(3):
                    tile = ref[STEPS + y, c * ratio + r, at_own : at_own + GROUP]
                    out[pl.ds(c * plane + r * ny + y, GROUP, stride=stride)] = tile if factor is None else tile * factor


def call(kernel, name, outs, specs, scratch, about_us, args, vmem=VMEM_LIMIT):
    return pl.pallas_call(
        kernel,
        out_shape=outs,
        in_specs=specs,
        out_specs=tuple(pl.BlockSpec(memory_space=pltpu.VMEM) for _ in outs),
        scratch_shapes=scratch,
        compiler_params=pltpu.CompilerParams(vmem_limit_bytes=vmem),
        cost_estimate=pl.CostEstimate(flops=int(about_us * 1e9), bytes_accessed=0, transcendentals=0),
        name=name,
    )(*args)


def body(sizes, e_init, h_init, eps_levels, region_gain, region_labels, kl_blocks, kl_modes, source_z, source_amp):
    n_gx, n_gy, n_mode = sizes
    _, nx, ny, nz = e_init.shape
    assert n_gy == 4 and n_mode == 4 and ny == TILE and nx <= 16 and nx % GROUP == 0 and nx >= STEPS and ny < STEPS < 2 * ny
    ratio, plane = nx // GROUP, nx * ny
    size = (nx, ny)
    vmem, smem, hbm = (pl.BlockSpec(memory_space=s) for s in (pltpu.VMEM, pltpu.SMEM, pltpu.HBM))
    f32 = lambda *shape: jax.ShapeDtypeStruct(shape, F32)
    i16 = lambda *shape: jax.ShapeDtypeStruct(shape, jnp.int16)

    def over_xy(block, dx, flip):
        route = [
            (gx * n_gy + gy, (gx + dx) % n_gx * n_gy + (gy ^ flip))
            for gx in range(n_gx)
            for gy in range(n_gy)
        ]
        return lax.ppermute(block, ("gx", "gy"), route)

    def over_mode(block, flip):
        return lax.ppermute(block, "mode", [(i, i ^ flip) for i in range(n_mode)])

    me = lax.axis_index("mode").astype(jnp.int32).reshape(1)
    parity = (lax.axis_index("gy") % 2).astype(jnp.int32).reshape(1)
    packed, own, own_part, near_part, tables, far_parts = call(
        functools.partial(pack_kernel, size), "pack",
        (
            i16(info_row(size) + 16, nz), f32(info_row(size) + 16, nz), f32(plane, nz), f32(plane, nz), f32(TILE, nz),
            i16(2 * (plane + 16), nz),
        ),
        [smem] + [hbm] * 9,
        [pltpu.SMEM(a.shape, a.dtype) for a in (kl_modes, eps_levels, region_gain)]
        + [pltpu.VMEM((3 * plane, nz), F32)] * 2
        + [pltpu.VMEM((plane, nz), jnp.int32), pltpu.VMEM((kl_blocks.shape[0] * plane, nz), kl_blocks.dtype)]
        + [pltpu.VMEM((ny, nx), jnp.int32), pltpu.VMEM((ny, nx), F32), pltpu.VMEM((2 * plane, nz), F32)]
        + [pltpu.SemaphoreType.DMA((9,))],
        1.5,
        (
            me,
            *(
                pltpu.with_memory_space_constraint(a, pltpu.HBM)
                for a in (
                    kl_modes, eps_levels, region_gain, e_init.reshape(-1, nz), h_init.reshape(-1, nz),
                    region_labels.reshape(-1, nz), kl_blocks.reshape(-1, nz), source_z.T, source_amp.T,
                )
            ),
        ),
    )

    moves_x = [0, -1] if n_gx == 2 else [0, -1, 1]
    order = (0, 1) if n_gx == 2 else (2, 0, 1, 1)
    groups = GROUP * len(order)

    def gather(block):
        near = [block] + [over_xy(block, dx, 0) for dx in moves_x[1:]]
        far = [over_xy(block, dx, 2) for dx in moves_x]
        return near, far

    far_parts = over_mode(far_parts, 1)
    (near_part,) = call(
        functools.partial(half_kernel, size), "half",
        (i16(plane + 16, nz),), [vmem] * 2, [pltpu.VMEM((16, nz), F32)], 0.2, (near_part, far_parts),
    )
    near, far = gather(packed)
    near_part = over_mode(near_part, 2)
    *corners, near_part = lax.optimization_barrier((*far[1:], near_part))

    def with_core(near, far):
        got = near + far
        sent = over_xy(jnp.concatenate(got, 0), 0, 1)
        rows = got[0].shape[0]
        other = [sent[rows * i : rows * i + rows] for i in range(len(got))]
        other_near, other_far = other[: len(near)], other[len(near) :]
        return [b for four in zip(near, other_near, far, other_far) for b in four]

    deps_packed, deps_own = call(
        functools.partial(sum_kernel, size), "sum",
        (i16(plane + 16, nz), f32(plane, nz)), [vmem] * 3,
        [pltpu.VMEM((3 * plane, nz), F32)] + [pltpu.VMEM((16, nz), F32)] * 2,
        1.2, (own_part, far_parts, near_part),
    )
    *sides, middle, deps_packed = lax.optimization_barrier((*near[1:], far[0], deps_packed))
    near, far = [packed, *sides], [middle, *corners]
    blocks = with_core(near, far)
    rows = ny + 2 * STEPS
    counts = [rows_of(step, ny)[1] - rows_of(step, ny)[0] for step in range(STEPS)]
    moved = [sum(counts[:FIRST_STEPS]), sum(counts[FIRST_STEPS:])]
    plane_shape, field_shape = (rows, ratio, groups, nz), (rows, 3 * ratio, groups, nz)
    deps_near, deps_far = gather(deps_packed)
    coef, gain, moves_first, electric, magnetic, profile = call(
        functools.partial(base_kernel, size, order), "base",
        (f32(*plane_shape), f32(*plane_shape), f32(moved[0], *field_shape[1:]), f32(*field_shape), f32(*field_shape), f32(*plane_shape)),
        [smem] + [vmem] * (1 + len(blocks)),
        [pltpu.VMEM((12 * ratio * len(set(order)) * TILE, nz), F32), pltpu.VMEM((4 * len(order) * nx, nz), F32)],
        3.5, (parity, tables, own, *blocks[1:]),
    )
    deps_far, deps_near, coef, gain, moves_first = lax.optimization_barrier(
        (deps_far[::-1], deps_near, coef, gain, moves_first)
    )
    deps = with_core(deps_near, deps_far[::-1])
    (moves_later,) = call(
        functools.partial(later_kernel, size), "later",
        (f32(moved[1], *field_shape[1:]),), [vmem] * 4, [pltpu.VMEM(field_shape, F32)] * 2,
        1.5, (coef, profile, electric, magnetic),
    )
    out_e, out_h = call(
        functools.partial(tangent_kernel, size, order), "tangent",
        (f32(3 * plane, nz), f32(3 * plane, nz)),
        [smem] + [vmem] * (4 + len(deps)),
        [pltpu.VMEM(field_shape, F32)] * 2
        + [pltpu.VMEM(plane_shape, F32), pltpu.VMEM((16 * (len(deps) - 1), nz), F32)],
        4.0, (parity, coef, gain, moves_first, moves_later, deps_own, *deps[1:]),
    )
    shape = (1, 3, nx, ny, nz)
    return out_e.reshape(shape), out_h.reshape(shape)


def solution(mesh):
    placed = (
        P(None, "gx", "gy", None),
        P(None, "gx", "gy", None),
        P(),
        P(),
        P("gx", "gy", None),
        P("mode", "gx", "gy", None),
        P(),
        P("gx", "gy"),
        P("gx", "gy"),
    )
    return jax.shard_map(
        functools.partial(body, tuple(mesh.shape[a] for a in ("gx", "gy", "mode"))),
        mesh=mesh,
        in_specs=placed,
        out_specs=(P("mode", None, "gx", "gy", None), P("mode", None, "gx", "gy", None)),
        check_vma=False,
    )
```

```python
import functools
import math

import jax
import jax.numpy as jnp
from jax import lax
from jax.experimental import pallas as pl
from jax.experimental.pallas import tpu as pltpu
from jax.sharding import PartitionSpec as P

STEPS = 10
DT_STEP = 0.99 / math.sqrt(3.0)
OMEGA_FREQ = 0.7

GROUP = 4
TILE = 8
FULL = 32000.0
FINE = 256.0
FIRST_STEPS = 4
SCALE_AT = 4 * 8
CHUNK = 26
F32 = jnp.float32
VMEM_LIMIT = 24 * 1024 * 1024


def iota(axis, rows=TILE):
    return lax.broadcasted_iota(jnp.int32, (rows, 128), axis)


def scale_code(largest):
    return jnp.clip(jnp.ceil(jnp.log2(largest) * FINE) + 1.0, -FULL, FULL)


def to_codes(values, code):
    return jnp.round(values * (jnp.exp2(code * (-1.0 / FINE)) * FULL))


def scale_of(code):
    return jnp.exp2(code * (1.0 / FINE)) * (1.0 / FULL)


def narrow(tiles):
    return jnp.concatenate(tiles, 0).astype(jnp.int32).astype(jnp.int16)


def wide(codes):
    return codes.astype(jnp.int32).astype(F32)


def lane(tile, at):
    return jnp.broadcast_to(tile[:, at : at + 1], tile.shape)


def code_tiles(total, k, codes):
    rows, coded = iota(0, 16), []
    for i in range(2):
        tile = total[TILE * i : TILE * i + TILE]
        code = scale_code(jnp.max(jnp.abs(tile), axis=(0, 1), keepdims=True))
        coded.append(to_codes(tile, code))
        codes = jnp.where(rows == 2 * k + i, code, codes)
    return narrow(coded), codes


def decoded(part, at, scales, k):
    coded = wide(part[at + 16 * k : at + 16 * k + 16])
    return [coded[TILE * i : TILE * i + TILE] * scales[2 * k + i : 2 * k + i + 1] for i in range(2)]


def half_kernel(size, near_part, far_parts, part, scales):
    plane = size[0] * size[1]
    codes = jnp.zeros((16, 128), F32)
    scales[...] = scale_of(wide(far_parts[2 * plane + 16 :]))
    for k in range(plane // 16):
        total = near_part[16 * k : 16 * k + 16] + jnp.concatenate(decoded(far_parts, plane + 16, scales, k), 0)
        part[16 * k : 16 * k + 16], codes = code_tiles(total, k, codes)
    part[plane:] = narrow([codes])


def field_rows(size, y, r):
    nx, ny = size
    ratio = nx // GROUP
    second, third = 16 * ny * ratio, 24 * ny * ratio
    return (
        (y * ratio + r) * 16,
        second + (y // 2 * ratio + r) * 16 + y % 2 * TILE,
        third + (y // 4 * ratio + r) * 16 + y % 4 * GROUP,
    )


def info_row(size):
    nx, ny = size
    return 28 * ny * (nx // GROUP)


def pack_kernel(
    size, me, modes_at, levels_at, gains_at, e_at, h_at, labels_at, kl_at, z_at, amp_at,
    packed, own, own_part, near_part, tables, far_parts, *rest,
):
    nx, ny = size
    modes, levels, gains, e, h, labels, kl, source_z, source_amp, label_rows, sems = rest
    ratio, plane, stride = nx // GROUP, nx * ny, nx // GROUP * ny
    ends = zip(
        (modes_at, levels_at, gains_at, kl_at, e_at, h_at, labels_at, z_at, amp_at),
        (modes, levels, gains, kl, e, h, labels, source_z, source_amp),
    )
    copies = [pltpu.make_async_copy(there, here, sems.at[i]) for i, (there, here) in enumerate(ends)]
    for copy in copies:
        copy.start()
    label_rows[plane:] = jnp.zeros((plane, 128), F32)
    for copy in copies[:4]:
        copy.wait()
    for i in range(3):
        at = slice(i, i + 1)
        tables[at] = jnp.full((1, 128), DT_STEP * DT_STEP) / jnp.full((1, 128), levels[i])
        tables[slice(i + 3, i + 4)] = jnp.full((1, 128), gains[i]) / jnp.full((1, 128), levels[i])
    tables[6:8] = jnp.zeros((2, 128), F32)
    low, lanes = iota(0) < GROUP, iota(1)

    blocks = kl.shape[0] // plane
    weights = [
        [(modes[me[0] * blocks + j] == (me[0] ^ d)).astype(F32) for j in range(blocks)] for d in (0, 2, 1, 3)
    ]
    codes = [jnp.zeros((16, 128), F32) for _ in range(2)]
    for k in range(plane // 16):
        tiles = [kl[j * plane + 16 * k : j * plane + 16 * k + 16].astype(F32) for j in range(blocks)]
        for d in range(4):
            total = sum(weights[d][j] * tiles[j] for j in range(blocks))
            if d < 2:
                (own_part, near_part)[d][16 * k : 16 * k + 16] = total
            else:
                first = (plane + 16) * (d - 2) + 16 * k
                far_parts[first : first + 16], codes[d - 2] = code_tiles(total, k, codes[d - 2])
    for i in range(2):
        first = (plane + 16) * i + plane
        far_parts[first : first + 16] = narrow([codes[i]])

    for copy in copies[4:]:
        copy.wait()
    label_rows[:plane] = labels[...].astype(F32)
    heights_of = source_z[...].astype(F32)
    amps_of = source_amp[...]
    info = jnp.zeros((TILE, 128), F32)
    rows = iota(0)
    for r in range(ratio):
        labels_held = []
        for y in range(ny):
            at = r * ny + y
            tiles = [e[pl.ds(at, TILE, stride=stride)], h[pl.ds(at, TILE, stride=stride)]]
            e_last = e[pl.ds(at + plane, TILE, stride=stride)]
            h_last = h[pl.ds(at + plane, TILE, stride=stride)]
            tiles.append(jnp.where(low, pltpu.roll(e_last, GROUP, 0), h_last))
            coded = []
            for i, tile in enumerate(tiles):
                code = scale_code(jnp.max(jnp.abs(tile), axis=(0, 1), keepdims=True))
                coded.append(to_codes(tile, code))
                info = jnp.where((rows == y) & (lanes == SCALE_AT + i * ratio + r), code, info)
            first, second, third = field_rows(size, y, r)
            packed[first : first + 16] = narrow(coded[:2])
            own[first : first + TILE] = tiles[0]
            own[first + TILE : first + 16] = tiles[1]
            own[second : second + TILE] = tiles[2]
            labels_held.append(label_rows[pl.ds(at, TILE, stride=stride)])
            if y % 2 == 0:
                last_even = coded[2]
                continue
            packed[second - TILE : second + TILE] = narrow([last_even, coded[2]])
            pair = jnp.where(low, labels_held[-2], pltpu.roll(labels_held[-1], GROUP, 0))
            labels_held[-2:] = [pair]
            third = third // TILE * TILE
            own[third : third + TILE] = pair
            if len(labels_held) == 2:
                packed[third - TILE : third + TILE] = narrow(labels_held)
                labels_held = []
    amp_codes = scale_code(jnp.abs(amps_of))
    sources = [heights_of, to_codes(amps_of, amp_codes), amp_codes, amps_of]
    sources = jnp.concatenate([jnp.concatenate(sources, 0), jnp.zeros((4 * ny, 128 - nx), F32)], 1)
    sources = jnp.concatenate([sources, jnp.zeros((128 - 4 * ny, 128), F32)], 0).T[:16]
    lanes16 = iota(1, 16)
    last = info_row(size)
    info = jnp.concatenate([info, jnp.zeros((TILE, 128), F32)], 0)
    packed[last : last + 16] = jnp.where(lanes16 < 3 * ny, sources, info).astype(jnp.int32).astype(jnp.int16)
    own[last : last + 16] = jnp.where(lanes16 < ny, sources, pltpu.roll(sources, 128 - 2 * ny, 1))


def sum_kernel(size, own_part, far_parts, near_part, packed, own, total, far_scales, near_scales):
    nx, ny = size
    ratio, plane, stride = nx // GROUP, nx * ny, nx // GROUP * ny
    far_scales[...] = scale_of(wide(far_parts[plane : plane + 16]))
    near_scales[...] = scale_of(wide(near_part[plane:]))
    total[:plane] = jnp.zeros((plane, 128), F32)
    total[2 * plane :] = jnp.zeros((plane, 128), F32)
    for k in range(plane // 16):
        both = zip(decoded(far_parts, 0, far_scales, k), decoded(near_part, 0, near_scales, k))
        for i, (far, near) in enumerate(both):
            at = 16 * k + TILE * i
            total[plane + at : plane + at + TILE] = own_part[at : at + TILE] + far + near
    low, rows16 = iota(0) < GROUP, iota(0, 16)
    codes = jnp.zeros((16, 128), F32)
    held = []
    for pair in range(ny // 2):
        for r in range(ratio):
            at = r * ny + 2 * pair
            even = total[pl.ds(plane + at, TILE, stride=stride)]
            odd = total[pl.ds(at + 1, TILE, stride=stride)]
            tile = jnp.where(low, even, odd)
            unit = pair * ratio + r
            own[TILE * unit : TILE * unit + TILE] = tile
            code = scale_code(jnp.max(jnp.abs(tile), axis=(0, 1), keepdims=True))
            codes = jnp.where(rows16 == unit, code, codes)
            held.append(to_codes(tile, code))
            if len(held) == 2:
                packed[TILE * (unit - 1) : TILE * (unit + 1)] = narrow(held)
                held = []
    packed[plane:] = narrow([codes])


def x_up(tiles):
    rows = tiles[0].shape[0]
    return tiles[1:] + [pltpu.roll(tiles[0], rows - 1, 0)]


def x_down(tiles):
    return [pltpu.roll(tiles[-1], 1, 0)] + tiles[:-1]


def z_up(tiles):
    last = iota(1, tiles[0].shape[0]) == 127
    return [jnp.where(last, 0.0, pltpu.roll(t, 127, 1)) for t in tiles]


def z_down(tiles):
    first = iota(1, tiles[0].shape[0]) == 0
    return [jnp.where(first, 0.0, pltpu.roll(t, 1, 1)) for t in tiles]


def add_curl_forward(magnetic, now, above):
    ex, ey, ez = now
    above_x, _, above_z = above
    ups = (z_up(ex), z_up(ey), x_up(ey), x_up(ez))
    out = [[], [], []]
    for r in range(len(ex)):
        curl = (
            (above_z[r] - ez[r]) - (ups[1][r] - ey[r]),
            (ups[0][r] - ex[r]) - (ups[3][r] - ez[r]),
            (ups[2][r] - ey[r]) - (above_x[r] - ex[r]),
        )
        for c in range(3):
            out[c].append(-curl[c] if magnetic is None else magnetic[c][r] - curl[c])
    return out


def curl_backward(now, below_x, below_z):
    hx, hy, hz = now
    downs = (z_down(hx), z_down(hy), x_down(hy), x_down(hz))
    out = [[], [], []]
    for r in range(len(hx)):
        out[0].append((hz[r] - below_z[r]) - (hy[r] - downs[1][r]))
        out[1].append((hx[r] - downs[0][r]) - (hz[r] - downs[3][r]))
        out[2].append((hy[r] - downs[2][r]) - (hx[r] - below_x[r]))
    return out


def load_row(ref, at, ratio):
    return [[ref[at, c * ratio + r] for r in range(ratio)] for c in range(3)]


def store_row(ref, at, row):
    ratio = len(row[0])
    for c in range(3):
        for r in range(ratio):
            ref[at, c * ratio + r] = row[c][r]


def flat(row):
    return [t for tiles in row for t in tiles]


def rows_of(step, ny):
    return step + 1, ny + 2 * STEPS - 1 - step


def chunks(first, end):
    count = -(-(end - first) // CHUNK)
    cuts = [first + (end - first) * i // count for i in range(count + 1)]
    return [range(*cut) for cut in zip(cuts, cuts[1:])]


def places(parity, ny):
    upper, lower = STEPS + ny, STEPS - ny
    one = jnp.where(parity == 0, upper, lower)
    three = jnp.where(parity == 0, lower, upper)
    over = STEPS - ny
    return (
        ((0, ny, STEPS),),
        ((0, ny, one),),
        ((ny - over, over, 0), (0, over, STEPS + 2 * ny)),
        ((0, ny, three),),
    )


def halves(pairs, low):
    one, two = pairs
    return [
        jnp.where(low, one, pltpu.roll(two, GROUP, 0)),
        jnp.where(low, pltpu.roll(one, GROUP, 0), two),
    ]


def base_kernel(size, order, parity, tables, own, *rest):
    nx, ny = size
    ratio = nx // GROUP
    blocks, rest = rest[:-8], rest[-8:]
    coef, gain_out, moves, electric, magnetic, profile, scales, sources = rest
    blocks = (own,) + blocks
    low, lanes = iota(0) < GROUP, iota(1)
    table = [jnp.broadcast_to(tables[i : i + 1], (TILE, 128)) for i in range(6)]

    def pick(label, first):
        return jnp.where(label < 0.5, table[first], jnp.where(label < 1.5, table[first + 1], table[first + 2]))

    last = info_row(size)
    def prepare(y_block):
        found = {}
        for x_block in set(order):
            block = 4 * x_block + y_block
            if block == 0:
                found[x_block] = own[last : last + 16]
                continue
            info = wide(blocks[block][last : last + 16])
            scale = scale_of(info)
            for i in range(3 * ratio):
                at = (3 * ratio * block + i) * TILE
                scales[at : at + TILE] = lane(scale[:TILE], SCALE_AT + i)
            amps = info * pltpu.roll(scale, 128 - ny, 1)
            found[x_block] = jnp.where(iota(1, 16) < ny, info, amps)
        for i, x_block in enumerate(order):
            at = (y_block * len(order) + i) * nx
            sources[at : at + nx] = found[x_block][:nx]

    def load_pair(block, pair, r):
        out = []
        for y in (2 * pair, 2 * pair + 1):
            first, second, third = field_rows(size, y, r)
            if block == 0:
                tiles = [own[first : first + TILE], own[first + TILE : first + 16], own[second : second + TILE]]
            else:
                both = wide(blocks[block][first : first + 16])
                at = second // 16 * 16
                ends = wide(blocks[block][at : at + 16])[second - at : second - at + TILE]
                tiles = [both[:TILE], both[TILE:], ends]
                rows = [((3 * block + i) * ratio + r) * TILE + y for i in range(3)]
                tiles = [t * scales[row : row + 1] for t, row in zip(tiles, rows)]
            out.append(tiles)
        third = field_rows(size, 2 * pair, r)[2]
        if block == 0:
            return out, own[third : third + TILE]
        at = third // 16 * 16
        return out, wide(blocks[block][at : at + 16])[third - at : third - at + TILE]

    def unpack(y_block, pair, to):
        for r in range(ratio):
            held = {x: load_pair(4 * x + y_block, pair, r) for x in set(order)}
            for i, y in enumerate((2 * pair, 2 * pair + 1)):
                outs = []
                for k in range(0, len(order), 2):
                    one, two = order[k], order[k + 1]
                    tiles = [halves((held[one][0][i][j], held[two][0][i][j]), low) for j in range(3)]
                    (ex, ey), (hx, hy), (ez, hz) = tiles
                    label = halves((held[one][1], held[two][1]), low)[i]
                    at = (y_block * len(order) + k) * nx
                    source = sources[pl.ds(at + r, TILE, stride=ratio)]
                    height, amp = lane(source, y), lane(source, ny + y)
                    outs.append(
                        [
                            ex * DT_STEP, ey * DT_STEP, ez * DT_STEP, hx, hy, hz, pick(label, 0), pick(label, 3),
                            jnp.where(lanes.astype(F32) == height, amp, 0.0),
                        ]
                    )
                for j in range(9):
                    tile = jnp.concatenate([o[j] for o in outs], 0) if len(outs) > 1 else outs[0][j]
                    if j < 3:
                        electric[to + i, j * ratio + r] = tile
                    elif j < 6:
                        magnetic[to + i, (j - 3) * ratio + r] = tile
                    else:
                        (coef, gain_out, profile)[j - 6][to + i, r] = tile

    for y_block, pieces in enumerate(places(parity[0], ny)):
        prepare(y_block)
        for first, count, to in pieces:
            for j in range(0, count, 2):
                unpack(y_block, (first + j) // 2, to + j)

    base_steps(size, range(FIRST_STEPS), coef, profile, moves, (electric, magnetic), (electric, magnetic))


def later_kernel(size, coef, profile, electric, magnetic, moves, electric_held, magnetic_held):
    base_steps(
        size, range(FIRST_STEPS, STEPS), coef, profile, moves, (electric, magnetic), (electric_held, magnetic_held)
    )


def base_steps(size, steps, coef, profile, moves, fields, held):
    nx, ny = size
    ratio = nx // GROUP
    to_electric, to_magnetic = held
    moved = 0
    for step in steps:
        electric, magnetic = fields if step == steps[0] else held
        wave = math.cos(OMEGA_FREQ * (step + 0.5) * DT_STEP)
        first, end = rows_of(step, ny)
        now = load_row(electric, first - 1, ratio)
        above = load_row(electric, first, ratio)
        new = add_curl_forward(load_row(magnetic, first - 1, ratio), now, above)
        below_x, below_z = new[0], new[2]
        for run in chunks(first, end):
            field = [above] + [load_row(electric, at + 1, ratio) for at in run]
            above = field[-1]
            new = [
                add_curl_forward(load_row(magnetic, at, ratio), field[i], field[i + 1])
                for i, at in enumerate(run)
            ]
            for i, at in enumerate(run):
                drive = curl_backward(new[i], below_x, below_z)
                below_x, below_z = new[i][0], new[i][2]
                drive[2] = [d + wave * profile[at, r] for r, d in enumerate(drive[2])]
                change = [[coef[at, r] * drive[c][r] for r in range(ratio)] for c in range(3)]
                store_row(moves, at - first + moved, change)
                if step < STEPS - 1:
                    store_row(to_magnetic, at, new[i])
                    store_row(
                        to_electric, at,
                        [[p + q for p, q in zip(field[i][c], change[c])] for c in range(3)],
                    )
        moved += end - first


def tangent_kernel(size, order, parity, coef, gain, moves_first, moves_later, own, *rest):
    nx, ny = size
    ratio, plane = nx // GROUP, nx * ny
    n_blocks = 4 * len(set(order)) - 1
    blocks, rest = (own,) + rest[:n_blocks], rest[n_blocks:]
    out_e, out_h, electric, magnetic, weight, scales = rest
    low = iota(0) < GROUP

    for i, block in enumerate(blocks[1:]):
        scales[16 * i : 16 * i + 16] = scale_of(wide(block[plane : plane + 16]))

    def unpack(y_block, pair, to, wanted):
        loaded = {}
        for x_block in order:
            i = 4 * x_block + y_block
            if x_block in loaded:
                continue
            tiles = []
            for r in range(ratio):
                unit = pair * ratio + r
                if i == 0:
                    tiles.append(own[TILE * unit : TILE * unit + TILE])
                else:
                    at = TILE * unit // 16 * 16
                    both = wide(blocks[i][at : at + 16])
                    half = TILE * unit - at
                    row = 16 * (i - 1) + unit
                    tiles.append(both[half : half + TILE] * scales[row : row + 1])
            loaded[x_block] = tiles
        for r in range(ratio):
            outs = [
                halves((loaded[order[k]][r], loaded[order[k + 1]][r]), low)
                for k in range(0, len(order), 2)
            ]
            for i in wanted:
                tile = jnp.concatenate([o[i] for o in outs], 0) if len(outs) > 1 else outs[0][i]
                weight[to + i, r] = tile * gain[to + i, r]

    for y_block, pieces in enumerate(places(parity[0], ny)):
        for first, count, to in pieces:
            for j in range(0, count, 2):
                unpack(y_block, (first + j) // 2, to + j, (0, 1))

    moved = 0
    for step in range(STEPS):
        first, end = rows_of(step, ny)
        if step == FIRST_STEPS:
            moved = 0
        moves = moves_first if step < FIRST_STEPS else moves_later
        shift = moved - first
        if step == 0:

            for at in range(first, end):
                change = load_row(moves, at + shift, ratio)
                store_row(electric, at, [[-(weight[at, r] * change[c][r]) for r in range(ratio)] for c in range(3)])
        else:

            def old(at, step=step):
                return load_row(magnetic, at, ratio) if step > 1 else None

            now = load_row(electric, first - 1, ratio)
            above = load_row(electric, first, ratio)
            new = add_curl_forward(old(first - 1), now, above)

            below_x, below_z = new[0], new[2]
            for run in chunks(first, end):
                field = [above] + [load_row(electric, at + 1, ratio) for at in run]
                above = field[-1]
                new = [add_curl_forward(old(at), field[i], field[i + 1]) for i, at in enumerate(run)]
                for i, at in enumerate(run):
                    curl = curl_backward(new[i], below_x, below_z)
                    below_x, below_z = new[i][0], new[i][2]
                    change = load_row(moves, at + shift, ratio)
                    store_row(magnetic, at, new[i])
                    store_row(
                        electric, at,
                        [
                            [
                                field[i][c][r] + (coef[at, r] * curl[c][r] - weight[at, r] * change[c][r])
                                for r in range(ratio)
                            ]
                            for c in range(3)
                        ],
                    )
        moved += end - first

    at_own = GROUP * order.index(0)
    stride = ratio * ny
    for y in range(ny):
        for r in range(ratio):
            for out, ref, factor in ((out_e, electric, 1.0 / DT_STEP), (out_h, magnetic, None)):
                for c in range(3):
                    tile = ref[STEPS + y, c * ratio + r, at_own : at_own + GROUP]
                    out[pl.ds(c * plane + r * ny + y, GROUP, stride=stride)] = tile if factor is None else tile * factor


def call(kernel, name, outs, specs, scratch, about_us, args, vmem=VMEM_LIMIT):
    return pl.pallas_call(
        kernel,
        out_shape=outs,
        in_specs=specs,
        out_specs=tuple(pl.BlockSpec(memory_space=pltpu.VMEM) for _ in outs),
        scratch_shapes=scratch,
        compiler_params=pltpu.CompilerParams(vmem_limit_bytes=vmem),
        cost_estimate=pl.CostEstimate(flops=int(about_us * 1e9), bytes_accessed=0, transcendentals=0),
        name=name,
    )(*args)


def body(sizes, e_init, h_init, eps_levels, region_gain, region_labels, kl_blocks, kl_modes, source_z, source_amp):
    n_gx, n_gy, n_mode = sizes
    _, nx, ny, nz = e_init.shape
    assert n_gy == 4 and n_mode == 4 and ny == TILE and nx <= 16 and nx % GROUP == 0 and nx >= STEPS and ny < STEPS < 2 * ny
    ratio, plane = nx // GROUP, nx * ny
    size = (nx, ny)
    vmem, smem, hbm = (pl.BlockSpec(memory_space=s) for s in (pltpu.VMEM, pltpu.SMEM, pltpu.HBM))
    f32 = lambda *shape: jax.ShapeDtypeStruct(shape, F32)
    i16 = lambda *shape: jax.ShapeDtypeStruct(shape, jnp.int16)

    def over_xy(block, dx, flip):
        route = [
            (gx * n_gy + gy, (gx + dx) % n_gx * n_gy + (gy ^ flip))
            for gx in range(n_gx)
            for gy in range(n_gy)
        ]
        return lax.ppermute(block, ("gx", "gy"), route)

    def over_mode(block, flip):
        return lax.ppermute(block, "mode", [(i, i ^ flip) for i in range(n_mode)])

    me = lax.axis_index("mode").astype(jnp.int32).reshape(1)
    parity = (lax.axis_index("gy") % 2).astype(jnp.int32).reshape(1)
    packed, own, own_part, near_part, tables, far_parts = call(
        functools.partial(pack_kernel, size), "pack",
        (
            i16(info_row(size) + 16, nz), f32(info_row(size) + 16, nz), f32(plane, nz), f32(plane, nz), f32(TILE, nz),
            i16(2 * (plane + 16), nz),
        ),
        [smem] + [hbm] * 9,
        [pltpu.SMEM(a.shape, a.dtype) for a in (kl_modes, eps_levels, region_gain)]
        + [pltpu.VMEM((3 * plane, nz), F32)] * 2
        + [pltpu.VMEM((plane, nz), jnp.int32), pltpu.VMEM((kl_blocks.shape[0] * plane, nz), kl_blocks.dtype)]
        + [pltpu.VMEM((ny, nx), jnp.int32), pltpu.VMEM((ny, nx), F32), pltpu.VMEM((2 * plane, nz), F32)]
        + [pltpu.SemaphoreType.DMA((9,))],
        1.5,
        (
            me,
            *(
                pltpu.with_memory_space_constraint(a, pltpu.HBM)
                for a in (
                    kl_modes, eps_levels, region_gain, e_init.reshape(-1, nz), h_init.reshape(-1, nz),
                    region_labels.reshape(-1, nz), kl_blocks.reshape(-1, nz), source_z.T, source_amp.T,
                )
            ),
        ),
    )

    moves_x = [0, -1] if n_gx == 2 else [0, -1, 1]
    order = (0, 1) if n_gx == 2 else (2, 0, 1, 1)
    groups = GROUP * len(order)

    def gather(block):
        near = [block] + [over_xy(block, dx, 0) for dx in moves_x[1:]]
        far = [over_xy(block, dx, 2) for dx in moves_x]
        return near, far

    far_parts = over_mode(far_parts, 1)
    (near_part,) = call(
        functools.partial(half_kernel, size), "half",
        (i16(plane + 16, nz),), [vmem] * 2, [pltpu.VMEM((16, nz), F32)], 0.2, (near_part, far_parts),
    )
    near, far = gather(packed)
    near_part = over_mode(near_part, 2)
    *corners, near_part = lax.optimization_barrier((*far[1:], near_part))

    def with_core(near, far):
        got = near + far
        sent = over_xy(jnp.concatenate(got, 0), 0, 1)
        rows = got[0].shape[0]
        other = [sent[rows * i : rows * i + rows] for i in range(len(got))]
        other_near, other_far = other[: len(near)], other[len(near) :]
        return [b for four in zip(near, other_near, far, other_far) for b in four]

    deps_packed, deps_own = call(
        functools.partial(sum_kernel, size), "sum",
        (i16(plane + 16, nz), f32(plane, nz)), [vmem] * 3,
        [pltpu.VMEM((3 * plane, nz), F32)] + [pltpu.VMEM((16, nz), F32)] * 2,
        1.2, (own_part, far_parts, near_part),
    )
    *sides, middle, deps_packed = lax.optimization_barrier((*near[1:], far[0], deps_packed))
    near, far = [packed, *sides], [middle, *corners]
    blocks = with_core(near, far)
    rows = ny + 2 * STEPS
    counts = [rows_of(step, ny)[1] - rows_of(step, ny)[0] for step in range(STEPS)]
    moved = [sum(counts[:FIRST_STEPS]), sum(counts[FIRST_STEPS:])]
    plane_shape, field_shape = (rows, ratio, groups, nz), (rows, 3 * ratio, groups, nz)
    deps_near, deps_far = gather(deps_packed)
    coef, gain, moves_first, electric, magnetic, profile = call(
        functools.partial(base_kernel, size, order), "base",
        (f32(*plane_shape), f32(*plane_shape), f32(moved[0], *field_shape[1:]), f32(*field_shape), f32(*field_shape), f32(*plane_shape)),
        [smem] + [vmem] * (1 + len(blocks)),
        [pltpu.VMEM((12 * ratio * len(set(order)) * TILE, nz), F32), pltpu.VMEM((4 * len(order) * nx, nz), F32)],
        3.5, (parity, tables, own, *blocks[1:]),
    )
    deps_far, deps_near, coef, gain, moves_first = lax.optimization_barrier(
        (deps_far[::-1], deps_near, coef, gain, moves_first)
    )
    deps = with_core(deps_near, deps_far[::-1])
    (moves_later,) = call(
        functools.partial(later_kernel, size), "later",
        (f32(moved[1], *field_shape[1:]),), [vmem] * 4, [pltpu.VMEM(field_shape, F32)] * 2,
        1.5, (coef, profile, electric, magnetic),
    )
    out_e, out_h = call(
        functools.partial(tangent_kernel, size, order), "tangent",
        (f32(3 * plane, nz), f32(3 * plane, nz)),
        [smem] + [vmem] * (4 + len(deps)),
        [pltpu.VMEM(field_shape, F32)] * 2
        + [pltpu.VMEM(plane_shape, F32), pltpu.VMEM((16 * (len(deps) - 1), nz), F32)],
        4.0, (parity, coef, gain, moves_first, moves_later, deps_own, *deps[1:]),
    )
    shape = (1, 3, nx, ny, nz)
    return out_e.reshape(shape), out_h.reshape(shape)


def solution(mesh):
    placed = (
        P(None, "gx", "gy", None),
        P(None, "gx", "gy", None),
        P(),
        P(),
        P("gx", "gy", None),
        P("mode", "gx", "gy", None),
        P(),
        P("gx", "gy"),
        P("gx", "gy"),
    )
    return jax.shard_map(
        functools.partial(body, tuple(mesh.shape[a] for a in ("gx", "gy", "mode"))),
        mesh=mesh,
        in_specs=placed,
        out_specs=(P("mode", None, "gx", "gy", None), P("mode", None, "gx", "gy", None)),
        check_vma=False,
    )
```
